256 devices in a mesh: dp: 16 (over x_hi, y, core), proto: 16 (over x_lo, z).
Axes of the slice: x: 4 (x_hi: 2, x_lo: 2; x = x_hi * 2 + x_lo), y: 4, z: 8, core: 2. Of those that a mesh axis runs over, the one named last changes fastest.
Arguments:
- student_cls: bfloat16 [8192, 1536], P('dp', 'proto'), may hold values from -56 to 56
- teacher_cls: bfloat16 [8192, 1536], P('dp', 'proto'), may hold values from -56 to 56
- student_gain: float32 [1536], replicated, may hold values from 0.1 to 1.9
- teacher_gain: float32 [1536], replicated, may hold values from 0.1 to 1.9
- student_proj: bfloat16 [1536, 384], P('proto'), may hold values from -1 to 1
- teacher_proj: float32 [1536, 384], P('proto'), may hold values from -1 to 1
- prototypes: bfloat16 [65536, 384], P('proto'), may hold values from -1 to 1
- partner: int32 [8192], P('dp'), may hold values from 0 to 8191, as said below
Outputs:
- crop_loss: float32 [8192], P('dp')
- grad_proj: float32 [1536, 384], P('proto')
- grad_protos: float32 [65536, 384], P(('proto', 'dp'))
- teacher_next: float32 [1536, 384], P('proto')
The draws below stay inside these ranges and needn't reach their ends.
Inputs may be any that keep to these rules, and one draw needn't show every extreme that they name: partner pairs the crops: partner[partner[i]] = i and partner[i] != i; crop i's partner lies among the 512 crops of the dp index half the dp axis away from i's.
All inputs are finite; a program needn't handle non-finite values.
Results may differ from the reference program's by a relative error of at most 0.02.
Values may be sent and summed in bfloat16 or wider, within the bound.
No kernel may reach another device: no remote copies, remote signals or barrier semaphores. Data moves between devices by JAX's collectives and lax.ppermute only.
A program may use at most 128 MiB of HBM per device.

```python
import jax
import jax.numpy as jnp
from jax import lax

D = 1536
P_SIZE = 384
K = 65536
ITERS = 3
CROPS_DEV = 512
CROPS = 8192
N_DP = 16


def skewed_labels(key, count):
    first, second, third, fourth = jax.random.split(key, 4)
    relabel = jax.random.permutation(first, 16).astype(jnp.int32)
    spread_label = jax.random.randint(second, (count,), 0, 16)
    common_label = jax.random.randint(third, (count,), 0, 4)
    choose = jax.random.randint(fourth, (count,), 0, 2)
    return jnp.take(relabel, jnp.where(choose == 0, common_label, spread_label).astype(jnp.int32))


def crop_layout(key):
    pair_key = jax.random.fold_in(key, 71)
    label_key = jax.random.fold_in(key, 73)
    half_axis = N_DP // 2
    half_crops = CROPS // 2
    block_keys = jax.random.split(pair_key, half_axis)
    within = jax.vmap(lambda one: jax.random.permutation(one, CROPS_DEV))(block_keys).astype(jnp.int32)
    first = jnp.arange(half_crops, dtype=jnp.int32)
    group = first // CROPS_DEV
    second = half_crops + group * CROPS_DEV + within.reshape(half_crops)
    partner = jnp.zeros((CROPS,), jnp.int32)
    partner = partner.at[first].set(second)
    partner = partner.at[second].set(first)
    band_key, mix_key, pick_key = jax.random.split(label_key, 3)
    lower = group * 16 // half_axis
    upper = jnp.maximum((group + 1) * 16 // half_axis, lower + 1)
    band_label = jax.random.randint(band_key, (half_crops,), lower, upper) % 16
    mixed_label = skewed_labels(mix_key, half_crops)
    pick = jax.random.randint(pick_key, (half_crops,), 0, 4)
    image_label = jnp.where(pick == 0, mixed_label, band_label).astype(jnp.int32)
    labels = jnp.zeros((CROPS,), jnp.int32)
    labels = labels.at[first].set(image_label)
    labels = labels.at[second].set(image_label)
    return (partner, labels)


def shared_projection(key):
    return jax.random.normal(jax.random.fold_in(key, 91), (D, P_SIZE), jnp.float32) / D ** 0.5


def spike_rows(labels, strength):
    columns = jnp.arange(D, dtype=jnp.int32)
    marked = (columns[None, :] == labels[:, None] * (D // 16)).astype(jnp.float32)
    return marked * strength


def draw_student_cls(key, part):
    partner, labels = crop_layout(key)
    key = jax.random.fold_in(key, 11)
    first = jax.random.fold_in(key, 0)
    third = jax.random.fold_in(key, 2)
    column_scale = jnp.exp(jax.random.uniform(first, (D,), jnp.float32, -1.15, 1.15))
    peak = 1.1 * D ** 0.5
    values = jnp.clip(jax.random.normal(third, (CROPS, D), jnp.float32), -4.0, 4.0) * column_scale[None, :] + spike_rows(labels, peak)
    return jnp.clip(values, -56.0, 56.0).astype(jnp.bfloat16)


def draw_teacher_cls(key, part):
    partner, labels = crop_layout(key)
    key = jax.random.fold_in(key, 23)
    first = jax.random.fold_in(key, 0)
    third = jax.random.fold_in(key, 2)
    column_scale = jnp.exp(jax.random.uniform(first, (D,), jnp.float32, -1.15, 1.15))
    peak = 1.1 * D ** 0.5
    values = jnp.clip(jax.random.normal(third, (CROPS, D), jnp.float32), -4.0, 4.0) * column_scale[None, :] + spike_rows(labels, peak)
    return jnp.clip(values, -56.0, 56.0).astype(jnp.bfloat16)


def draw_student_proj(key, part):
    common = shared_projection(key)
    key = jax.random.fold_in(key, 31)
    own = jax.random.normal(key, (D, P_SIZE), jnp.float32) / D ** 0.5
    return jnp.clip(common + 0.5 * own, -1.0, 1.0).astype(jnp.bfloat16)


def draw_teacher_proj(key, part):
    common = shared_projection(key)
    key = jax.random.fold_in(key, 29)
    own = jax.random.normal(key, (D, P_SIZE), jnp.float32) / D ** 0.5
    return jnp.clip(common + 0.5 * own, -1.0, 1.0)


def draw_prototypes(key, part):
    common = shared_projection(key)
    key = jax.random.fold_in(key, 37)
    first, second = jax.random.split(key, 2)
    labels = skewed_labels(first, K)
    centre = jnp.take(common, labels * (D // 16), axis=0) * (D / P_SIZE) ** 0.5
    noise = jax.random.normal(second, (K, P_SIZE), jnp.float32)
    values = 0.55 * centre + 0.85 * noise / P_SIZE ** 0.5
    return jnp.clip(values, -1.0, 1.0).astype(jnp.bfloat16)


def draw_partner(key, part):
    partner, labels = crop_layout(key)
    return partner


def setup_inputs(seed: int = 0) -> dict:
    key_of = jax.random.split(jax.random.key(seed), 9)
    student_cls = draw_student_cls(jax.random.fold_in(key_of[8], 71), 0)
    teacher_cls = draw_teacher_cls(jax.random.fold_in(key_of[8], 71), 0)
    student_gain = jnp.clip(1.0 + 0.18 * jax.random.normal(key_of[2], (D,), jnp.float32), 0.1, 1.9)
    teacher_gain = jnp.clip(1.0 + 0.18 * jax.random.normal(key_of[3], (D,), jnp.float32), 0.1, 1.9)
    student_proj = draw_student_proj(jax.random.fold_in(key_of[8], 71), 0)
    teacher_proj = draw_teacher_proj(jax.random.fold_in(key_of[8], 71), 0)
    prototypes = draw_prototypes(jax.random.fold_in(key_of[8], 71), 0)
    partner = draw_partner(jax.random.fold_in(key_of[8], 71), 0)
    return dict(student_cls=student_cls, teacher_cls=teacher_cls, student_gain=student_gain, teacher_gain=teacher_gain, student_proj=student_proj, teacher_proj=teacher_proj, prototypes=prototypes, partner=partner)


EPSILON = 1e-06
TEACHER_TEMP = 0.07
STUDENT_TEMP = 0.1
MOMENTUM = 0.994

def layer_norm(features, gain):
    values = features.astype(jnp.float32)
    center = lax.optimization_barrier(jnp.sum(values, axis=1)) / D
    spread = lax.optimization_barrier(jnp.sum(values * values, axis=1)) / D - center * center
    normed = (values - center[:, None]) * lax.rsqrt(spread[:, None] + EPSILON) * gain[None, :]
    return normed.astype(jnp.bfloat16)

def unit_rows(values):
    factor = lax.rsqrt(lax.optimization_barrier(jnp.sum(values * values, axis=1, keepdims=True)) + EPSILON)
    return (values * factor, factor)

def reference(student_cls, teacher_cls, student_gain, teacher_gain, student_proj, teacher_proj, prototypes, partner):
    student_normed = layer_norm(student_cls, student_gain)
    teacher_normed = layer_norm(teacher_cls, teacher_gain)
    student_hidden = jnp.dot(student_normed, student_proj, preferred_element_type=jnp.float32)
    teacher_hidden = jnp.dot(teacher_normed, teacher_proj.astype(jnp.bfloat16), preferred_element_type=jnp.float32)
    student_unit32, student_factor = unit_rows(student_hidden)
    student_unit = student_unit32.astype(jnp.bfloat16)
    teacher_unit32, teacher_factor = unit_rows(teacher_hidden)
    teacher_unit = teacher_unit32.astype(jnp.bfloat16)
    paired = jnp.take(teacher_unit, partner.astype(jnp.int32), axis=0)
    proto_unit32, proto_factor = unit_rows(prototypes.astype(jnp.float32))
    proto_unit = proto_unit32.astype(jnp.bfloat16)
    block_width = min(K, 4096)
    block_count = K // block_width
    blocks = proto_unit.reshape(block_count, block_width, P_SIZE)

    def energies(block):
        return jnp.exp(jnp.dot(paired, block.T, preferred_element_type=jnp.float32) / TEACHER_TEMP)
    crop_scale = jnp.ones((CROPS,), jnp.float32)
    proto_scale = jnp.ones((block_count, block_width), jnp.float32)
    for step in range(ITERS):
        current = crop_scale

        def sweep(total, block):
            energy = energies(block)
            scale = 1.0 / jnp.dot(current, energy, precision=lax.Precision.HIGHEST)
            return (total + jnp.dot(energy, scale, precision=lax.Precision.HIGHEST), scale)
        row_sums, proto_scale = lax.scan(sweep, jnp.zeros((CROPS,), jnp.float32), blocks)
        crop_scale = 1.0 / row_sums

    def block_codes(block, scale):
        return crop_scale[:, None] * energies(block) * scale[None, :]

    def block_logits(block):
        return jnp.dot(student_unit, block.T, preferred_element_type=jnp.float32) / STUDENT_TEMP

    def totals(pair):
        block, scale = pair
        codes = block_codes(block, scale)
        logits = block_logits(block)
        return (lax.optimization_barrier(jnp.sum(jnp.exp(logits), axis=1)), lax.optimization_barrier(jnp.sum(codes * logits, axis=1)))
    exp_parts, code_parts = lax.map(totals, (blocks, proto_scale))
    partition = lax.optimization_barrier(jnp.sum(exp_parts, axis=0))
    expected = lax.optimization_barrier(jnp.sum(code_parts, axis=0))
    crop_loss = jnp.log(partition) - expected

    def gradients(pair):
        block, scale = pair
        codes = block_codes(block, scale)
        logits = block_logits(block)
        score_grad = ((jnp.exp(logits) / partition[:, None] - codes) / STUDENT_TEMP).astype(jnp.bfloat16)
        embed_part = jnp.dot(score_grad, block, preferred_element_type=jnp.float32)
        grouped = score_grad.astype(jnp.float32).reshape(N_DP, CROPS_DEV, block_width)
        student_grouped = student_unit.astype(jnp.float32).reshape(N_DP, CROPS_DEV, P_SIZE)
        device_terms = jnp.einsum('gik,gip->gkp', grouped, student_grouped).astype(jnp.bfloat16)
        return (embed_part, lax.optimization_barrier(jnp.sum(device_terms.astype(jnp.float32), axis=0)))
    embed_parts, proto_parts = lax.map(gradients, (blocks, proto_scale))
    unit_grad = lax.optimization_barrier(jnp.sum(embed_parts, axis=0))
    proto_unit_grad = proto_parts.reshape(K, P_SIZE)
    grad_protos = proto_factor * (proto_unit_grad - proto_unit32 * lax.optimization_barrier(jnp.sum(proto_unit32 * proto_unit_grad, axis=1, keepdims=True)))
    hidden_grad = (student_factor * (unit_grad - student_unit32 * lax.optimization_barrier(jnp.sum(student_unit32 * unit_grad, axis=1, keepdims=True)))).astype(jnp.bfloat16)
    grad_proj = jnp.dot(student_normed.T, hidden_grad, preferred_element_type=jnp.float32)
    teacher_next = MOMENTUM * teacher_proj + (1.0 - MOMENTUM) * student_proj.astype(jnp.float32)
    return (crop_loss, grad_proj, grad_protos, teacher_next)
```

```python
import jax
import jax.numpy as jnp
from jax import lax
from jax.sharding import PartitionSpec as P

D = 1536
ITERS = 3


EPSILON = 1e-06
TEACHER_TEMP = 0.07
STUDENT_TEMP = 0.1
MOMENTUM = 0.994
BF16 = jnp.bfloat16
F32 = jnp.float32


def contract_last(left, right):
    return lax.dot_general(left, right, (((1,), (1,)), ((), ())), preferred_element_type=F32)


def contract_first(left, right):
    return lax.dot_general(left, right, (((0,), (0,)), ((), ())), preferred_element_type=F32)


def unit_rows(values):
    factor = lax.rsqrt(jnp.sum(values * values, axis=1, keepdims=True) + EPSILON)
    return (values * factor, factor)


def exchanged(blocks, axis):
    return lax.all_to_all(blocks, axis, 0, 0)


def from_all(value, axis):
    count = lax.axis_size(axis)
    return exchanged(jnp.broadcast_to(value[None], (count,) + value.shape), axis)


def three_terms(value):
    high = value.astype(BF16)
    rest = value - high.astype(F32)
    middle = rest.astype(BF16)
    low = (rest - middle.astype(F32)).astype(BF16)
    return high, middle, low


def swapped(value, axis, bit):
    count = lax.axis_size(axis)
    return lax.ppermute(value, axis, [(one, one ^ bit) for one in range(count)])


def partial_hidden(features, gain, weight):
    scaled = (gain[:, None] * weight.astype(BF16).astype(F32)).astype(BF16)
    share = jnp.dot(features, scaled, preferred_element_type=F32)
    column = jnp.sum(scaled.astype(F32), axis=0)
    values = features.astype(F32)
    return share, column, jnp.sum(values, axis=1), jnp.sum(values * values, axis=1)


def center_and_scale(first, second):
    center = first / D
    return center, lax.rsqrt(second / D - center * center + EPSILON)


def summed_protos(part):
    me = lax.axis_index("dp")
    core, along_y, along_x = me % 2, (me // 2) % 4, me // 8
    rows = part.shape[0] // 16
    blocks = part.reshape(2, 4, 2, rows, part.shape[1])
    keep = lax.dynamic_index_in_dim(blocks, core, 2, False)
    give = lax.dynamic_index_in_dim(blocks, 1 - core, 2, False)
    blocks = (keep.astype(F32) + swapped(give, "dp", 1).astype(F32)).astype(BF16)
    yield None
    total = lax.dynamic_index_in_dim(blocks, along_y, 1, False).astype(F32)
    for step in range(1, 4):
        give = lax.dynamic_index_in_dim(blocks, (along_y + step) % 4, 1, False)
        pairs = [(one, (one & 9) | ((one + 2 * step) & 6)) for one in range(16)]
        total = total + lax.ppermute(give, "dp", pairs).astype(F32)
    blocks = total.astype(BF16)
    yield None
    keep = lax.dynamic_index_in_dim(blocks, along_x, 0, False)
    give = lax.dynamic_index_in_dim(blocks, 1 - along_x, 0, False)
    yield keep.astype(F32) + swapped(give, "dp", 8).astype(F32)


def body(
    student_cls,
    teacher_cls,
    student_gain,
    teacher_gain,
    student_proj,
    teacher_proj,
    prototypes,
    partner,
):
    crops, width = student_cls.shape
    parts = lax.axis_size("proto")
    own = crops // parts
    size = student_proj.shape[1]
    start = lax.axis_index("proto") * width
    opposite = swapped(teacher_cls, "dp", 8)
    gain_s = lax.dynamic_slice_in_dim(student_gain, start, width)
    gain_t = lax.dynamic_slice_in_dim(teacher_gain, start, width)

    share, column, first, second = partial_hidden(student_cls, gain_s, student_proj)
    extra = jnp.concatenate(
        [
            jnp.broadcast_to(column, (parts, 1, size)),
            jnp.pad(
                jnp.stack([first.reshape(parts, own), second.reshape(parts, own)], 1),
                ((0, 0), (0, 5), (0, size - own)),
            ),
        ],
        1,
    )
    packed = jnp.concatenate([share.reshape(parts, own, size), extra], 1)
    packed = packed.reshape(parts * (own + 8), size)
    packed = lax.psum_scatter(packed, "proto", scatter_dimension=0, tiled=True)
    student_center, student_scale = center_and_scale(
        packed[own + 1, :own, None], packed[own + 2, :own, None]
    )
    student_hidden = student_scale * (packed[:own] - student_center * packed[own][None])
    student_unit32, student_factor = unit_rows(student_hidden)
    student_unit = lax.all_gather(student_unit32.astype(BF16), "proto", axis=0, tiled=True)

    share, column, first, second = partial_hidden(opposite, gain_t, teacher_proj)
    small = jnp.pad(
        jnp.stack(three_terms(jnp.stack([first, second])), 0).reshape(6, parts, own).transpose(1, 0, 2).reshape(parts, 1, 6 * own),
        ((0, 0), (0, 0), (0, size - 6 * own)),
    )
    columns = jnp.broadcast_to(jnp.stack(three_terms(column))[None], (parts, 3, size))
    packed = jnp.concatenate([share.astype(BF16).reshape(parts, own, size), columns, small], 1)
    packed = jnp.sum(exchanged(packed, "proto").astype(F32), axis=0)
    sums = jnp.sum(packed[own + 3, : 6 * own].reshape(3, 2, own), axis=0)
    teacher_center, teacher_scale = center_and_scale(sums[0][:, None], sums[1][:, None])
    teacher_hidden = teacher_scale * (
        packed[:own] - teacher_center * jnp.sum(packed[own : own + 3], axis=0)[None]
    )
    teacher_unit = unit_rows(teacher_hidden)[0].astype(BF16)
    teacher_all = from_all(teacher_unit, "proto").reshape(crops, size)
    pick = (partner[:, None] % crops == jnp.arange(crops, dtype=jnp.int32)[None]).astype(BF16)
    paired = jnp.dot(pick, teacher_all, preferred_element_type=F32).astype(BF16)

    proto_unit32, proto_factor = unit_rows(prototypes.astype(F32))
    proto_unit = proto_unit32.astype(BF16)
    protos = proto_unit.shape[0]
    energy = jnp.exp(contract_last(paired, proto_unit) / TEACHER_TEMP)
    row = jnp.ones((crops,), F32)
    for step in range(ITERS):
        sums = jnp.sum(energy * row[:, None], axis=0)
        col = 1.0 / jnp.sum(from_all(sums.reshape(protos // 128, 128), "dp"), axis=0).reshape(protos)
        scaled = energy * col[None, :]
        if step < ITERS - 1:
            sums = jnp.sum(scaled, axis=1)
            row = 1.0 / jnp.sum(from_all(sums.reshape(crops // 128, 128), "proto"), axis=0).reshape(crops)
    logits = contract_last(student_unit, proto_unit) / STUDENT_TEMP
    exponent = jnp.exp(logits)
    sums = jnp.stack([jnp.sum(scaled, axis=1), jnp.sum(exponent, axis=1), jnp.sum(scaled * logits, axis=1)])
    sums = jnp.sum(from_all(sums.reshape(3 * crops // 128, 128), "proto"), axis=0).reshape(3, crops)
    row = 1.0 / sums[0]
    partition = sums[1]
    crop_loss = jnp.log(partition) - sums[2] * row
    score_grad = (
        exponent * (1.0 / (partition * STUDENT_TEMP))[:, None] - scaled * (row / STUDENT_TEMP)[:, None]
    ).astype(BF16)

    stages = summed_protos(contract_first(score_grad, student_unit).astype(BF16))
    next(stages)
    unit_grad = jnp.dot(score_grad, proto_unit, preferred_element_type=F32).astype(BF16)
    unit_grad = jnp.sum(exchanged(unit_grad.reshape(parts, own, size), "proto").astype(F32), axis=0)
    hidden_grad = student_factor * (
        unit_grad - student_unit32 * jnp.sum(student_unit32 * unit_grad, axis=1, keepdims=True)
    )
    sent = (hidden_grad * student_scale).astype(BF16)
    moved = jnp.stack(three_terms(jnp.sum(student_center * sent.astype(F32), axis=0)))
    next(stages)
    packed = from_all(jnp.concatenate([sent, moved], 0), "proto")
    moved = jnp.sum(packed[:, own:].astype(F32), axis=(0, 1))
    sent = packed[:, :own].reshape(crops, size)
    share = gain_s[:, None] * (contract_first(student_cls, sent) - moved[None])
    proto_unit_grad = next(stages)
    grad_proj = jnp.sum(from_all(share.astype(BF16), "dp").astype(F32), axis=0)

    count = protos // lax.axis_size("dp")
    own_start = lax.axis_index("dp") * count
    own_unit, own_factor = unit_rows(
        lax.dynamic_slice_in_dim(prototypes, own_start, count, 0).astype(F32)
    )
    grad_protos = own_factor * (
        proto_unit_grad - own_unit * jnp.sum(own_unit * proto_unit_grad, axis=1, keepdims=True)
    )
    teacher_next = MOMENTUM * teacher_proj + (1.0 - MOMENTUM) * student_proj.astype(F32)
    return (crop_loss, grad_proj, grad_protos, teacher_next)


def solution(mesh):
    placed = (
        P("dp", "proto"),
        P("dp", "proto"),
        P(),
        P(),
        P("proto", None),
        P("proto", None),
        P("proto", None),
        P("dp"),
    )
    return jax.shard_map(
        body,
        mesh=mesh,
        in_specs=placed,
        out_specs=(P("dp"), P("proto", None), P(("proto", "dp"), None), P("proto", None)),
        check_vma=False,
    )
```

```python
import jax
import jax.numpy as jnp
from jax import lax
from jax.sharding import PartitionSpec as P

D = 1536
ITERS = 3


EPSILON = 1e-06
TEACHER_TEMP = 0.07
STUDENT_TEMP = 0.1
MOMENTUM = 0.994
BF16 = jnp.bfloat16
F32 = jnp.float32


def contract_last(left, right):
    return lax.dot_general(left, right, (((1,), (1,)), ((), ())), preferred_element_type=F32)


def contract_first(left, right):
    return lax.dot_general(left, right, (((0,), (0,)), ((), ())), preferred_element_type=F32)


def unit_rows(values):
    factor = lax.rsqrt(jnp.sum(values * values, axis=1, keepdims=True) + EPSILON)
    return (values * factor, factor)


def exchanged(blocks, axis):
    return lax.all_to_all(blocks, axis, 0, 0)


def from_all(value, axis):
    count = lax.axis_size(axis)
    return exchanged(jnp.broadcast_to(value[None], (count,) + value.shape), axis)


def three_terms(value):
    high = value.astype(BF16)
    rest = value - high.astype(F32)
    middle = rest.astype(BF16)
    low = (rest - middle.astype(F32)).astype(BF16)
    return high, middle, low


def swapped(value, axis, bit):
    count = lax.axis_size(axis)
    return lax.ppermute(value, axis, [(one, one ^ bit) for one in range(count)])


def partial_hidden(features, gain, weight):
    scaled = (gain[:, None] * weight.astype(BF16).astype(F32)).astype(BF16)
    share = jnp.dot(features, scaled, preferred_element_type=F32)
    column = jnp.sum(scaled.astype(F32), axis=0)
    values = features.astype(F32)
    return share, column, jnp.sum(values, axis=1), jnp.sum(values * values, axis=1)


def center_and_scale(first, second):
    center = first / D
    return center, lax.rsqrt(second / D - center * center + EPSILON)


def packed_shares(features, gain, weight, parts):
    crops, size = features.shape[0], weight.shape[1]
    own = crops // parts
    share, column, first, second = partial_hidden(features, gain, weight)
    sums = jnp.stack(three_terms(jnp.stack([first, second])))
    sums = sums.reshape(6, parts, own).transpose(1, 0, 2).reshape(parts, 1, 6 * own)
    sums = jnp.pad(sums, ((0, 0), (0, 0), (0, size - 6 * own)))
    columns = jnp.broadcast_to(jnp.stack(three_terms(column))[None], (parts, 3, size))
    return jnp.concatenate([share.astype(BF16).reshape(parts, own, size), columns, sums], 1)


def summed_hidden(packed):
    own = packed.shape[1] - 4
    packed = jnp.sum(packed.astype(F32), axis=0)
    sums = jnp.sum(packed[own + 3, : 6 * own].reshape(3, 2, own), axis=0)
    center, scale = center_and_scale(sums[0][:, None], sums[1][:, None])
    column = jnp.sum(packed[own : own + 3], axis=0)[None]
    return scale * (packed[:own] - center * column), center, scale


def summed_protos(part):
    me = lax.axis_index("dp")
    core, along_y, along_x = me % 2, (me // 2) % 4, me // 8
    rows = part.shape[0] // 16
    blocks = part.reshape(2, 4, 2, rows, part.shape[1])
    keep = lax.dynamic_index_in_dim(blocks, core, 2, False)
    give = lax.dynamic_index_in_dim(blocks, 1 - core, 2, False)
    blocks = (keep.astype(F32) + swapped(give, "dp", 1).astype(F32)).astype(BF16)
    yield None
    total = lax.dynamic_index_in_dim(blocks, along_y, 1, False).astype(F32)
    for step in range(1, 4):
        give = lax.dynamic_index_in_dim(blocks, (along_y + step) % 4, 1, False)
        pairs = [(one, (one & 9) | ((one + 2 * step) & 6)) for one in range(16)]
        total = total + lax.ppermute(give, "dp", pairs).astype(F32)
    blocks = total.astype(BF16)
    yield None
    keep = lax.dynamic_index_in_dim(blocks, along_x, 0, False)
    give = lax.dynamic_index_in_dim(blocks, 1 - along_x, 0, False)
    yield keep.astype(F32) + swapped(give, "dp", 8).astype(F32)


def body(
    student_cls,
    teacher_cls,
    student_gain,
    teacher_gain,
    student_proj,
    teacher_proj,
    prototypes,
    partner,
):
    crops, width = student_cls.shape
    parts = lax.axis_size("proto")
    own = crops // parts
    size = student_proj.shape[1]
    start = lax.axis_index("proto") * width
    opposite = swapped(teacher_cls, "dp", 8)
    gain_s = lax.dynamic_slice_in_dim(student_gain, start, width)
    gain_t = lax.dynamic_slice_in_dim(teacher_gain, start, width)

    student_blocks = packed_shares(student_cls, gain_s, student_proj, parts)
    teacher_blocks = packed_shares(opposite, gain_t, teacher_proj, parts)
    teacher_hidden = summed_hidden(exchanged(teacher_blocks, "proto"))[0]
    teacher_unit = unit_rows(teacher_hidden)[0].astype(BF16)
    teacher_all = from_all(teacher_unit, "proto").reshape(crops, size)
    pick = (partner[:, None] % crops == jnp.arange(crops, dtype=jnp.int32)[None]).astype(BF16)
    paired = jnp.dot(pick, teacher_all, preferred_element_type=F32).astype(BF16)

    proto_unit32, proto_factor = unit_rows(prototypes.astype(F32))
    proto_unit = proto_unit32.astype(BF16)
    protos = proto_unit.shape[0]
    energy = jnp.exp(contract_last(paired, proto_unit) / TEACHER_TEMP)
    row = jnp.ones((crops,), F32)
    for step in range(ITERS):
        sums = jnp.sum(energy * row[:, None], axis=0).reshape(protos // 128, 128)
        if step == 0:
            sums, student_blocks = lax.optimization_barrier((sums, student_blocks))
            student_blocks = exchanged(student_blocks, "proto")
        if step == 1:
            sums, student_own = lax.optimization_barrier((sums, student_own))
            student_unit = from_all(student_own, "proto").reshape(crops, size)
        if step == 2:
            sums, student_unit = lax.optimization_barrier((sums, student_unit))
            exponent = jnp.exp(contract_last(student_unit, proto_unit) / STUDENT_TEMP)
            partition = jnp.sum(exponent, axis=1)
            exponent = exponent.astype(BF16)
            pulled = jnp.dot(exponent, proto_unit, preferred_element_type=F32)
        sums = from_all(sums, "dp")
        if step == 2:
            sums, exponent, partition, pulled = lax.optimization_barrier(
                (sums, exponent, partition, pulled)
            )
        col = 1.0 / jnp.sum(sums, axis=0).reshape(protos)
        scaled = energy * col[None, :]
        if step < ITERS - 1:
            sums = jnp.sum(scaled, axis=1)
            row = 1.0 / jnp.sum(from_all(sums.reshape(crops // 128, 128), "proto"), axis=0).reshape(crops)
        if step == 0:
            student_hidden, student_center, student_scale = summed_hidden(student_blocks)
            student_unit32, student_factor = unit_rows(student_hidden)
            student_own = student_unit32.astype(BF16)
    coded = jnp.dot(scaled.astype(BF16), proto_unit, preferred_element_type=F32)
    expected = jnp.sum(student_unit.astype(F32) * coded, axis=1) / STUDENT_TEMP
    sums = jnp.stack([jnp.sum(scaled, axis=1), partition, expected])
    sums = jnp.sum(from_all(sums.reshape(3 * crops // 128, 128), "proto"), axis=0).reshape(3, crops)
    row = 1.0 / sums[0]
    partition = sums[1]
    crop_loss = jnp.log(partition) - sums[2] * row
    wanted = (1.0 / (partition * STUDENT_TEMP))[:, None]
    given = (row / STUDENT_TEMP)[:, None]
    unit_grad = (pulled * wanted - coded * given).astype(BF16).reshape(parts, own, size)
    unit_grad = exchanged(unit_grad, "proto")
    score_grad = (exponent.astype(F32) * wanted - scaled * given).astype(BF16)

    stages = summed_protos(contract_first(score_grad, student_unit).astype(BF16))
    next(stages)
    unit_grad = jnp.sum(unit_grad.astype(F32), axis=0)
    hidden_grad = student_factor * (
        unit_grad - student_unit32 * jnp.sum(student_unit32 * unit_grad, axis=1, keepdims=True)
    )
    sent = (hidden_grad * student_scale).astype(BF16)
    moved = jnp.stack(three_terms(jnp.sum(student_center * sent.astype(F32), axis=0)))
    next(stages)
    packed = from_all(jnp.concatenate([sent, moved], 0), "proto")
    moved = jnp.sum(packed[:, own:].astype(F32), axis=(0, 1))
    sent = packed[:, :own].reshape(crops, size)
    share = gain_s[:, None] * (contract_first(student_cls, sent) - moved[None])
    proto_unit_grad = next(stages)
    grad_proj = jnp.sum(from_all(share.astype(BF16), "dp").astype(F32), axis=0)

    count = protos // lax.axis_size("dp")
    own_start = lax.axis_index("dp") * count
    own_unit, own_factor = unit_rows(
        lax.dynamic_slice_in_dim(prototypes, own_start, count, 0).astype(F32)
    )
    grad_protos = own_factor * (
        proto_unit_grad - own_unit * jnp.sum(own_unit * proto_unit_grad, axis=1, keepdims=True)
    )
    teacher_next = MOMENTUM * teacher_proj + (1.0 - MOMENTUM) * student_proj.astype(F32)
    return (crop_loss, grad_proj, grad_protos, teacher_next)


def solution(mesh):
    placed = (
        P("dp", "proto"),
        P("dp", "proto"),
        P(),
        P(),
        P("proto", None),
        P("proto", None),
        P("proto", None),
        P("dp"),
    )
    return jax.shard_map(
        body,
        mesh=mesh,
        in_specs=placed,
        out_specs=(P("dp"), P("proto", None), P(("proto", "dp"), None), P("proto", None)),
        check_vma=False,
    )
```

```python
import jax
import jax.numpy as jnp
from jax import lax
from jax.experimental import pallas as pl
from jax.experimental.pallas import tpu as pltpu
from jax.sharding import PartitionSpec as P

D = 1536
ITERS = 3


EPSILON = 1e-06
TEACHER_TEMP = 0.07
STUDENT_TEMP = 0.1
MOMENTUM = 0.994
BF16 = jnp.bfloat16
F32 = jnp.float32
LOG2E = 1.4426950408889634
BLOCK = 1024
LANES = 128


def contract_last(left, right):
    return lax.dot_general(left, right, (((1,), (1,)), ((), ())), preferred_element_type=F32)


def contract_first(left, right):
    return lax.dot_general(left, right, (((0,), (0,)), ((), ())), preferred_element_type=F32)


def unit_rows(values):
    factor = lax.rsqrt(jnp.sum(values * values, axis=1, keepdims=True) + EPSILON)
    return (values * factor, factor)


def exchanged(blocks, axis):
    return lax.all_to_all(blocks, axis, 0, 0)


def from_all(value, axis):
    count = lax.axis_size(axis)
    return exchanged(jnp.broadcast_to(value[None], (count,) + value.shape), axis)


def three_terms(value):
    high = value.astype(BF16)
    rest = value - high.astype(F32)
    middle = rest.astype(BF16)
    low = (rest - middle.astype(F32)).astype(BF16)
    return high, middle, low


def swapped(value, axis, bit):
    count = lax.axis_size(axis)
    return lax.ppermute(value, axis, [(one, one ^ bit) for one in range(count)])


def partial_hidden(features, gain, weight):
    scaled = (gain[:, None] * weight.astype(BF16).astype(F32)).astype(BF16)
    share = jnp.dot(features, scaled, preferred_element_type=F32)
    column = jnp.sum(scaled.astype(F32), axis=0)
    values = features.astype(F32)
    return share, column, jnp.sum(values, axis=1), jnp.sum(values * values, axis=1)


def center_and_scale(first, second):
    center = first / D
    return center, lax.rsqrt(second / D - center * center + EPSILON)


def packed_shares(features, gain, weight, parts):
    crops, size = features.shape[0], weight.shape[1]
    own = crops // parts
    share, column, first, second = partial_hidden(features, gain, weight)
    sums = jnp.stack(three_terms(jnp.stack([first, second])))
    sums = sums.reshape(6, parts, own).transpose(1, 0, 2).reshape(parts, 1, 6 * own)
    sums = jnp.pad(sums, ((0, 0), (0, 0), (0, size - 6 * own)))
    columns = jnp.broadcast_to(jnp.stack(three_terms(column))[None], (parts, 3, size))
    return jnp.concatenate([share.astype(BF16).reshape(parts, own, size), columns, sums], 1)


def summed_hidden(packed):
    own = packed.shape[1] - 4
    packed = jnp.sum(packed.astype(F32), axis=0)
    sums = jnp.sum(packed[own + 3, : 6 * own].reshape(3, 2, own), axis=0)
    center, scale = center_and_scale(sums[0][:, None], sums[1][:, None])
    column = jnp.sum(packed[own : own + 3], axis=0)[None]
    return scale * (packed[:own] - center * column)


def column_form(rows):
    return jnp.concatenate(
        [jnp.transpose(jnp.broadcast_to(rows[q : q + 1], (LANES, LANES))) for q in range(rows.shape[0])], 0
    )


def row_form(partial):
    return jnp.concatenate(
        [
            jnp.sum(jnp.transpose(partial[q * LANES : (q + 1) * LANES]), axis=0, keepdims=True)
            for q in range(partial.shape[0] // LANES)
        ],
        0,
    )


def stack_sum(ref):
    total = ref[0].astype(F32)
    for one in range(1, ref.shape[0]):
        total = total + ref[one].astype(F32)
    return total


def energy_kernel(pick_ref, teacher_ref, protos_ref, energy_ref, sums_ref, paired, held):
    step = pl.program_id(0)

    @pl.when(step == 0)
    def _():
        paired[...] = jnp.dot(pick_ref[...], teacher_ref[...], preferred_element_type=F32).astype(BF16)

    rows = []
    for part in range(BLOCK // 256):
        cut = slice(part * 256, part * 256 + 256)
        value = jnp.exp2(contract_last(paired[...], protos_ref[cut, :]) * (LOG2E / TEACHER_TEMP))
        energy_ref[:, cut] = value.astype(BF16)
        total = jnp.sum(value, axis=0, keepdims=True)
        rows += [total[:, :LANES], total[:, LANES:]]
    held[pl.ds(pl.multiple_of(step * 8, 8), 8), :] = jnp.concatenate(rows, 0)

    @pl.when(step == pl.num_programs(0) - 1)
    def _():
        for one in range(sums_ref.shape[0]):
            sums_ref[one] = held[...].astype(BF16)


def row_kernel(got_ref, energy_ref, sums_ref, scale, held):
    step = pl.program_id(0)

    @pl.when(step == 0)
    def _():
        scale[...] = 1.0 / stack_sum(got_ref)
        held[...] = jnp.zeros_like(held)

    start = step * 8
    for low in range(0, held.shape[0], LANES):
        cut = slice(low, low + LANES)
        total = held[cut, :]
        for tile in range(8):
            total = total + energy_ref[cut, tile * LANES : (tile + 1) * LANES].astype(F32) * scale[pl.ds(start + tile, 1), :]
        held[cut, :] = total

    @pl.when(step == pl.num_programs(0) - 1)
    def _():
        total = row_form(held[...])
        for one in range(sums_ref.shape[0]):
            sums_ref[one] = total


def col_kernel(got_ref, energy_ref, sums_ref, scale, held):
    step = pl.program_id(0)

    @pl.when(step == 0)
    def _():
        scale[...] = column_form(1.0 / stack_sum(got_ref))

    rows = []
    for tile in range(8):
        value = energy_ref[:, tile * LANES : (tile + 1) * LANES].astype(F32) * scale[...]
        rows.append(jnp.sum(value, axis=0, keepdims=True))
    held[pl.ds(pl.multiple_of(step * 8, 8), 8), :] = jnp.concatenate(rows, 0)

    @pl.when(step == pl.num_programs(0) - 1)
    def _():
        for one in range(sums_ref.shape[0]):
            sums_ref[one] = held[...].astype(BF16)


def student_kernel(student_ref, protos_ref, exponent_ref, pulled_ref, partition_ref, held):
    step = pl.program_id(0)

    @pl.when(step == 0)
    def _():
        held[...] = jnp.zeros_like(held)
        pulled_ref[...] = jnp.zeros_like(pulled_ref)

    for part in range(BLOCK // 256):
        cut = slice(part * 256, part * 256 + 256)
        value = jnp.exp2(contract_last(student_ref[...], protos_ref[cut, :]) * (LOG2E / STUDENT_TEMP))
        held[...] += value[:, :LANES] + value[:, LANES:]
        value = value.astype(BF16)
        exponent_ref[:, cut] = value
        pulled_ref[...] += jnp.dot(value, protos_ref[cut, :], preferred_element_type=F32)

    @pl.when(step == pl.num_programs(0) - 1)
    def _():
        partition_ref[...] = row_form(held[...])


def last_kernel(got_ref, partition_ref, energy_ref, student_ref, protos_ref, sums_ref, coded_ref, scale_ref, held):
    step = pl.program_id(0)

    @pl.when(step == 0)
    def _():
        scale_ref[...] = 1.0 / stack_sum(got_ref)
        held[...] = jnp.zeros_like(held)
        coded_ref[...] = jnp.zeros_like(coded_ref)

    start = step * 8
    for part in range(BLOCK // 256):
        left = energy_ref[:, part * 256 : part * 256 + LANES].astype(F32) * scale_ref[pl.ds(start + 2 * part, 1), :]
        right = energy_ref[:, part * 256 + LANES : part * 256 + 256].astype(F32) * scale_ref[pl.ds(start + 2 * part + 1, 1), :]
        held[...] += left + right
        value = jnp.concatenate([left.astype(BF16), right.astype(BF16)], 1)
        coded_ref[...] += jnp.dot(value, protos_ref[part * 256 : part * 256 + 256, :], preferred_element_type=F32)

    @pl.when(step == pl.num_programs(0) - 1)
    def _():
        value = student_ref[...].astype(F32) * coded_ref[...]
        expected = value[:, :LANES]
        for tile in range(1, value.shape[1] // LANES):
            expected = expected + value[:, tile * LANES : (tile + 1) * LANES]
        total = jnp.concatenate(
            [row_form(held[...]), partition_ref[...], row_form(expected) * (1.0 / STUDENT_TEMP)], 0
        )
        for one in range(sums_ref.shape[0]):
            sums_ref[one] = total


def unit_grad_kernel(got_ref, pulled_ref, coded_ref, grad_ref, loss_ref, wanted_ref, given_ref):
    total = stack_sum(got_ref)
    count = total.shape[0] // 3
    row = 1.0 / total[:count]
    partition = total[count : 2 * count]
    loss_ref[...] = jnp.log(partition) - total[2 * count :] * row
    wanted = column_form(1.0 / (partition * STUDENT_TEMP))
    given = column_form(row * (1.0 / STUDENT_TEMP))
    wanted_ref[...] = wanted
    given_ref[...] = given
    for tile in range(pulled_ref.shape[1] // LANES):
        cut = slice(tile * LANES, (tile + 1) * LANES)
        grad_ref[:, cut] = (pulled_ref[:, cut] * wanted - coded_ref[:, cut] * given).astype(BF16)


def proto_grad_kernel(core_ref, turned_ref, wanted_ref, given_ref, scale_ref, exponent_ref, energy_ref, keep_ref, give_ref):
    step = pl.program_id(0)
    core = core_ref[0]
    for out_ref, which in ((give_ref, 1 - core), (keep_ref, core)):
        parts = []
        for half in range(2):
            cut = pl.ds(pl.multiple_of(which * 256 + half * LANES, LANES), LANES)
            scale = scale_ref[pl.ds(step * 4 + which * 2 + half, 1), :]
            score = exponent_ref[:, cut].astype(F32) * wanted_ref[...] - energy_ref[:, cut].astype(F32) * scale * given_ref[...]
            parts.append(score.astype(BF16))
        out_ref[0] = jnp.dot(turned_ref[...], jnp.concatenate(parts, 1), preferred_element_type=F32).astype(BF16)


def whole(shape):
    return pl.BlockSpec(shape, lambda step: (0,) * len(shape))


def called(kernel, steps, ins, outs, scratch, flops=0, moved=0, exps=0):
    return pl.pallas_call(
        kernel,
        grid=(steps,),
        in_specs=ins,
        out_specs=[spec for _, spec in outs],
        out_shape=[shape for shape, _ in outs],
        scratch_shapes=scratch,
        compiler_params=pltpu.CompilerParams(
            dimension_semantics=("arbitrary",), vmem_limit_bytes=24 * 1024 * 1024
        ),
        cost_estimate=pl.CostEstimate(flops=flops, bytes_accessed=moved, transcendentals=exps),
    )


def array(shape, dtype):
    return jax.ShapeDtypeStruct(shape, dtype)


def make_calls(crops, protos, size, dps, parts):
    steps = protos // BLOCK
    lines, tiles = crops // LANES, protos // LANES
    across = pl.BlockSpec((crops, BLOCK), lambda step: (0, step))
    down = pl.BlockSpec((BLOCK, size), lambda step: (step, 0))
    matrix = crops * protos
    product = 2 * matrix * size
    col_sent = (array((dps, tiles, LANES), BF16), whole((dps, tiles, LANES)))
    row_sent = (array((parts, lines, LANES), F32), whole((parts, lines, LANES)))
    tall = pltpu.VMEM((crops, LANES), F32)
    short = pltpu.VMEM((tiles, LANES), F32)
    energy = called(
        energy_kernel, steps, [whole((crops, crops)), whole((crops, size)), down],
        [(array((crops, protos), BF16), across), col_sent],
        [pltpu.VMEM((crops, size), BF16), short], product, 2 * matrix, matrix,
    )
    rows = called(
        row_kernel, steps, [whole((dps, tiles, LANES)), across], [row_sent], [short, tall], 2 * matrix, 2 * matrix
    )
    cols = called(
        col_kernel, steps, [whole((parts, lines, LANES)), across], [col_sent], [tall, short], 2 * matrix, 2 * matrix
    )
    student = called(
        student_kernel, steps, [whole((crops, size)), down],
        [
            (array((crops, protos), BF16), across),
            (array((crops, size), F32), whole((crops, size))),
            (array((lines, LANES), F32), whole((lines, LANES))),
        ],
        [tall], 2 * product, 2 * matrix, matrix,
    )
    last = called(
        last_kernel, steps,
        [whole((dps, tiles, LANES)), whole((lines, LANES)), across, whole((crops, size)), down],
        [
            (array((parts, 3 * lines, LANES), F32), whole((parts, 3 * lines, LANES))),
            (array((crops, size), F32), whole((crops, size))),
            (array((tiles, LANES), F32), whole((tiles, LANES))),
        ],
        [tall], product, 2 * matrix,
    )
    unit_grad = called(
        unit_grad_kernel, 1,
        [whole((parts, 3 * lines, LANES)), whole((crops, size)), whole((crops, size))],
        [
            (array((crops, size), BF16), whole((crops, size))),
            (array((lines, LANES), F32), whole((lines, LANES))),
            (array((crops, LANES), F32), whole((crops, LANES))),
            (array((crops, LANES), F32), whole((crops, LANES))),
        ],
        [], 4 * crops * size, 10 * crops * size,
    )
    wide = protos // dps
    pair = pl.BlockSpec((crops, 2 * wide), lambda step: (0, step))
    block = (array((dps // 2, size, wide), BF16), pl.BlockSpec((1, size, wide), lambda step: (step, 0, 0)))
    proto_grad = called(
        proto_grad_kernel, dps // 2,
        [
            pl.BlockSpec(memory_space=pltpu.SMEM), whole((size, crops)), whole((crops, LANES)),
            whole((crops, LANES)), whole((tiles, LANES)), pair, pair,
        ],
        [block, block], [], product, 4 * matrix + 2 * protos * size,
    )
    return energy, rows, cols, student, last, unit_grad, proto_grad


def summed_protos(keep, give):
    me = lax.axis_index("dp")
    along_y, along_x = (me // 2) % 4, me // 8
    blocks = (keep.astype(F32) + swapped(give, "dp", 1).astype(F32)).astype(BF16)
    blocks = yield blocks.reshape((2, 4) + keep.shape[1:])
    total = lax.dynamic_index_in_dim(blocks, along_y, 1, False).astype(F32)
    for step in range(1, 4):
        give = lax.dynamic_index_in_dim(blocks, (along_y + step) % 4, 1, False)
        pairs = [(one, (one & 9) | ((one + 2 * step) & 6)) for one in range(16)]
        total = total + lax.ppermute(give, "dp", pairs).astype(F32)
    blocks = yield total.astype(BF16)
    keep = lax.dynamic_index_in_dim(blocks, along_x, 0, False)
    give = lax.dynamic_index_in_dim(blocks, 1 - along_x, 0, False)
    yield keep.astype(F32) + swapped(give, "dp", 8).astype(F32)


def body(
    student_cls,
    teacher_cls,
    student_gain,
    teacher_gain,
    student_proj,
    teacher_proj,
    prototypes,
    partner,
):
    crops, width = student_cls.shape
    parts = lax.axis_size("proto")
    own = crops // parts
    size = student_proj.shape[1]
    start = lax.axis_index("proto") * width
    opposite = swapped(teacher_cls, "dp", 8)
    gain_s = lax.dynamic_slice_in_dim(student_gain, start, width)
    gain_t = lax.dynamic_slice_in_dim(teacher_gain, start, width)

    weight = (gain_s[:, None] * student_proj.astype(F32)).astype(BF16)
    gathered = lax.all_gather(jnp.concatenate([student_cls.T, weight], 1), "proto", axis=0, tiled=True)
    teacher_blocks = packed_shares(opposite, gain_t, teacher_proj, parts)
    teacher_hidden = summed_hidden(exchanged(teacher_blocks, "proto"))
    teacher_unit = unit_rows(teacher_hidden)[0].astype(BF16)
    teacher_all = from_all(teacher_unit, "proto").reshape(crops, size)
    pick = (partner[:, None] % crops == jnp.arange(crops, dtype=jnp.int32)[None]).astype(BF16)
    proto_unit32, proto_factor = unit_rows(prototypes.astype(F32))
    proto_unit = proto_unit32.astype(BF16)
    protos = proto_unit.shape[0]
    energy_call, row_call, col_call, student_call, last_call, unit_grad_call, proto_grad_call = make_calls(
        crops, protos, size, lax.axis_size("dp"), parts
    )
    energy, sums = energy_call(pick, teacher_all, proto_unit)
    for step in range(ITERS - 1):
        (sums,) = row_call(exchanged(sums, "dp"), energy)
        (sums,) = col_call(exchanged(sums, "proto"), energy)

    sums, gathered = lax.optimization_barrier((sums, gathered))
    values = gathered[:, :crops].astype(F32)
    student_center, student_scale = center_and_scale(
        jnp.sum(values, axis=0)[:, None], jnp.sum(values * values, axis=0)[:, None]
    )
    weight = gathered[:, crops:]
    student_hidden = student_scale * (
        contract_first(gathered[:, :crops], weight) - student_center * jnp.sum(weight.astype(F32), axis=0)[None]
    )
    student_unit32, student_factor = unit_rows(student_hidden)
    student_unit = student_unit32.astype(BF16)
    exponent, pulled, partition = student_call(student_unit, proto_unit)
    sums = exchanged(sums, "dp")
    sums, exponent, pulled, partition = lax.optimization_barrier((sums, exponent, pulled, partition))
    sums, coded, scale = last_call(sums, partition, energy, student_unit, proto_unit)
    unit_grad, crop_loss, wanted, given = unit_grad_call(exchanged(sums, "proto"), pulled, coded)
    crop_loss = crop_loss.reshape(crops)
    unit_grad = exchanged(unit_grad.reshape(parts, own, size), "proto")
    core = (lax.axis_index("dp") % 2).reshape(1)
    keep, give = proto_grad_call(core, student_unit.T, wanted, given, scale, exponent, energy)
    stages = summed_protos(keep, give)
    blocks = next(stages)
    student_unit32, student_factor, student_center, student_scale = (
        lax.dynamic_slice_in_dim(value, lax.axis_index("proto") * own, own, 0)
        for value in (student_unit32, student_factor, student_center, student_scale)
    )
    unit_grad = jnp.sum(unit_grad.astype(F32), axis=0)
    hidden_grad = student_factor * (
        unit_grad - student_unit32 * jnp.sum(student_unit32 * unit_grad, axis=1, keepdims=True)
    )
    sent = (hidden_grad * student_scale).astype(BF16)
    moved = jnp.stack(three_terms(jnp.sum(student_center * sent.astype(F32), axis=0)))
    packed = jnp.concatenate([sent, moved], 0)
    packed, blocks = lax.optimization_barrier((packed, blocks))
    blocks = stages.send(blocks)
    packed = from_all(packed, "proto")
    moved = jnp.sum(packed[:, own:].astype(F32), axis=(0, 1))
    sent = packed[:, :own].reshape(crops, size)
    share = (gain_s[:, None] * (contract_first(student_cls, sent) - moved[None])).astype(BF16)
    share, blocks = lax.optimization_barrier((share, blocks))
    proto_unit_grad = stages.send(blocks).T
    grad_proj = jnp.sum(from_all(share, "dp").astype(F32), axis=0)

    count = protos // lax.axis_size("dp")
    own_start = lax.axis_index("dp") * count
    own_unit, own_factor = unit_rows(
        lax.dynamic_slice_in_dim(prototypes, own_start, count, 0).astype(F32)
    )
    grad_protos = own_factor * (
        proto_unit_grad - own_unit * jnp.sum(own_unit * proto_unit_grad, axis=1, keepdims=True)
    )
    teacher_next = MOMENTUM * teacher_proj + (1.0 - MOMENTUM) * student_proj.astype(F32)
    return (crop_loss, grad_proj, grad_protos, teacher_next)


def solution(mesh):
    placed = (
        P("dp", "proto"),
        P("dp", "proto"),
        P(),
        P(),
        P("proto", None),
        P("proto", None),
        P("proto", None),
        P("dp"),
    )
    return jax.shard_map(
        body,
        mesh=mesh,
        in_specs=placed,
        out_specs=(P("dp"), P("proto", None), P(("proto", "dp"), None), P("proto", None)),
        check_vma=False,
    )
```

```python
import jax
import jax.numpy as jnp
from jax import lax
from jax.experimental import pallas as pl
from jax.experimental.pallas import tpu as pltpu
from jax.sharding import PartitionSpec as P

D = 1536
ITERS = 3


EPSILON = 1e-06
TEACHER_TEMP = 0.07
STUDENT_TEMP = 0.1
MOMENTUM = 0.994
BF16 = jnp.bfloat16
F32 = jnp.float32
LOG2E = 1.4426950408889634
BLOCK = 1024
GRANT = 24 * 1024 * 1024
LANES = 128


def contract_last(left, right):
    return lax.dot_general(left, right, (((1,), (1,)), ((), ())), preferred_element_type=F32)


def contract_first(left, right):
    return lax.dot_general(left, right, (((0,), (0,)), ((), ())), preferred_element_type=F32)


def unit_rows(values):
    factor = lax.rsqrt(jnp.sum(values * values, axis=1, keepdims=True) + EPSILON)
    return (values * factor, factor)


def exchanged(blocks, axis):
    return lax.all_to_all(blocks, axis, 0, 0)


def from_all(value, axis):
    count = lax.axis_size(axis)
    return exchanged(jnp.broadcast_to(value[None], (count,) + value.shape), axis)


def three_terms(value):
    high = value.astype(BF16)
    rest = value - high.astype(F32)
    middle = rest.astype(BF16)
    low = (rest - middle.astype(F32)).astype(BF16)
    return high, middle, low


def swapped(value, axis, bit):
    count = lax.axis_size(axis)
    return lax.ppermute(value, axis, [(one, one ^ bit) for one in range(count)])


def partial_hidden(features, gain, weight):
    scaled = (gain[:, None] * weight.astype(BF16).astype(F32)).astype(BF16)
    share = jnp.dot(features, scaled, preferred_element_type=F32)
    column = jnp.sum(scaled.astype(F32), axis=0)
    values = features.astype(F32)
    return share, column, jnp.sum(values, axis=1), jnp.sum(values * values, axis=1)


def center_and_scale(first, second):
    center = first / D
    return center, lax.rsqrt(second / D - center * center + EPSILON)


def packed_shares(features, gain, weight, parts):
    crops, size = features.shape[0], weight.shape[1]
    own = crops // parts
    share, column, first, second = partial_hidden(features, gain, weight)
    sums = jnp.stack(three_terms(jnp.stack([first, second])))
    sums = sums.reshape(6, parts, own).transpose(1, 0, 2).reshape(parts, 1, 6 * own)
    sums = jnp.pad(sums, ((0, 0), (0, 0), (0, size - 6 * own)))
    columns = jnp.broadcast_to(jnp.stack(three_terms(column))[None], (parts, 3, size))
    return jnp.concatenate([share.astype(BF16).reshape(parts, own, size), columns, sums], 1)


def summed_hidden(packed):
    own = packed.shape[1] - 4
    packed = jnp.sum(packed.astype(F32), axis=0)
    sums = jnp.sum(packed[own + 3, : 6 * own].reshape(3, 2, own), axis=0)
    center, scale = center_and_scale(sums[0][:, None], sums[1][:, None])
    column = jnp.sum(packed[own : own + 3], axis=0)[None]
    return scale * (packed[:own] - center * column)


def column_form(rows):
    return jnp.concatenate(
        [jnp.transpose(jnp.broadcast_to(rows[q : q + 1], (LANES, LANES))) for q in range(rows.shape[0])], 0
    )


def row_form(partial):
    return jnp.concatenate(
        [
            jnp.sum(jnp.transpose(partial[q * LANES : (q + 1) * LANES]), axis=0, keepdims=True)
            for q in range(partial.shape[0] // LANES)
        ],
        0,
    )


def stack_sum(ref):
    total = ref[0].astype(F32)
    for one in range(1, ref.shape[0]):
        total = total + ref[one].astype(F32)
    return total


def energy_kernel(teacher_ref, protos_ref, energy_ref, sums_ref, held):
    step = pl.program_id(0)
    rows = []
    for part in range(BLOCK // 256):
        cut = slice(part * 256, part * 256 + 256)
        value = jnp.exp2(contract_last(teacher_ref[...], protos_ref[cut, :]) * (LOG2E / TEACHER_TEMP))
        energy_ref[:, cut] = value.astype(BF16)
        total = jnp.sum(value, axis=0, keepdims=True)
        rows += [total[:, :LANES], total[:, LANES:]]
    held[pl.ds(pl.multiple_of(step * 8, 8), 8), :] = jnp.concatenate(rows, 0)

    @pl.when(step == pl.num_programs(0) - 1)
    def _():
        for one in range(sums_ref.shape[0]):
            sums_ref[one] = held[...].astype(BF16)


def row_kernel(got_ref, energy_ref, sums_ref, scale, held):
    step = pl.program_id(0)

    @pl.when(step == 0)
    def _():
        scale[...] = 1.0 / stack_sum(got_ref)
        held[...] = jnp.zeros_like(held)

    start = step * 8
    for low in range(0, held.shape[0], LANES):
        cut = slice(low, low + LANES)
        total = held[cut, :]
        for tile in range(8):
            total = total + energy_ref[cut, tile * LANES : (tile + 1) * LANES].astype(F32) * scale[pl.ds(start + tile, 1), :]
        held[cut, :] = total

    @pl.when(step == pl.num_programs(0) - 1)
    def _():
        total = row_form(held[...])
        for one in range(sums_ref.shape[0]):
            sums_ref[one] = total


def col_kernel(got_ref, energy_ref, sums_ref, scale, held):
    step = pl.program_id(0)

    @pl.when(step == 0)
    def _():
        scale[...] = column_form(1.0 / stack_sum(got_ref))

    rows = []
    for tile in range(8):
        value = energy_ref[:, tile * LANES : (tile + 1) * LANES].astype(F32) * scale[...]
        rows.append(jnp.sum(value, axis=0, keepdims=True))
    held[pl.ds(pl.multiple_of(step * 8, 8), 8), :] = jnp.concatenate(rows, 0)

    @pl.when(step == pl.num_programs(0) - 1)
    def _():
        for one in range(sums_ref.shape[0]):
            sums_ref[one] = held[...].astype(BF16)


def student_kernel(student_ref, protos_ref, exponent_ref, pulled_ref, partition_ref, held):
    step = pl.program_id(0)

    @pl.when(step == 0)
    def _():
        held[...] = jnp.zeros_like(held)
        pulled_ref[...] = jnp.zeros_like(pulled_ref)

    for part in range(BLOCK // 256):
        cut = slice(part * 256, part * 256 + 256)
        value = jnp.exp2(contract_last(student_ref[...], protos_ref[cut, :]) * (LOG2E / STUDENT_TEMP))
        held[...] += value[:, :LANES] + value[:, LANES:]
        exponent_ref[:, cut] = value.astype(BF16)
    pulled_ref[...] += jnp.dot(exponent_ref[...], protos_ref[...], preferred_element_type=F32)

    @pl.when(step == pl.num_programs(0) - 1)
    def _():
        partition_ref[...] = row_form(held[...])


def last_kernel(got_ref, partition_ref, energy_ref, student_ref, protos_ref, sums_ref, coded_ref, scale_ref, held, scaled):
    step = pl.program_id(0)

    @pl.when(step == 0)
    def _():
        scale_ref[...] = 1.0 / stack_sum(got_ref)
        held[...] = jnp.zeros_like(held)
        coded_ref[...] = jnp.zeros_like(coded_ref)

    start = step * 8
    for part in range(BLOCK // 256):
        left = energy_ref[:, part * 256 : part * 256 + LANES].astype(F32) * scale_ref[pl.ds(start + 2 * part, 1), :]
        right = energy_ref[:, part * 256 + LANES : part * 256 + 256].astype(F32) * scale_ref[pl.ds(start + 2 * part + 1, 1), :]
        held[...] += left + right
        scaled[:, part * 256 : part * 256 + LANES] = left.astype(BF16)
        scaled[:, part * 256 + LANES : part * 256 + 256] = right.astype(BF16)
    coded_ref[...] += jnp.dot(scaled[...], protos_ref[...], preferred_element_type=F32)

    @pl.when(step == pl.num_programs(0) - 1)
    def _():
        value = student_ref[...].astype(F32) * coded_ref[...]
        expected = value[:, :LANES]
        for tile in range(1, value.shape[1] // LANES):
            expected = expected + value[:, tile * LANES : (tile + 1) * LANES]
        total = jnp.concatenate(
            [row_form(held[...]), partition_ref[...], row_form(expected) * (1.0 / STUDENT_TEMP)], 0
        )
        for one in range(sums_ref.shape[0]):
            sums_ref[one] = total


def unit_grad_kernel(got_ref, pulled_ref, coded_ref, grad_ref, loss_ref, wanted_ref, given_ref):
    total = stack_sum(got_ref)
    count = total.shape[0] // 3
    row = 1.0 / total[:count]
    partition = total[count : 2 * count]
    loss_ref[...] = jnp.log(partition) - total[2 * count :] * row
    wanted = column_form(1.0 / (partition * STUDENT_TEMP))
    given = column_form(row * (1.0 / STUDENT_TEMP))
    wanted_ref[...] = wanted
    given_ref[...] = given
    for tile in range(pulled_ref.shape[1] // LANES):
        cut = slice(tile * LANES, (tile + 1) * LANES)
        grad_ref[:, cut] = (pulled_ref[:, cut] * wanted - coded_ref[:, cut] * given).astype(BF16)


def proto_grad_kernel(core_ref, turned_ref, wanted_ref, given_ref, scale_ref, exponent_ref, energy_ref, out_ref):
    line = pl.program_id(0) * 4 + core_ref[0] * 2
    parts = []
    for half in range(2):
        cut = slice(half * LANES, half * LANES + LANES)
        scale = scale_ref[pl.ds(line + half, 1), :]
        score = exponent_ref[:, cut].astype(F32) * wanted_ref[...] - energy_ref[:, cut].astype(F32) * scale * given_ref[...]
        parts.append(score.astype(BF16))
    out_ref[0] = jnp.dot(turned_ref[...], jnp.concatenate(parts, 1), preferred_element_type=F32).astype(BF16)


def whole(shape):
    return pl.BlockSpec(shape, lambda step: (0,) * len(shape))


def called(kernel, steps, ins, outs, scratch, flops=0, moved=0, exps=0):
    return pl.pallas_call(
        kernel,
        grid=(steps,),
        in_specs=ins,
        out_specs=[spec for _, spec in outs],
        out_shape=[shape for shape, _ in outs],
        scratch_shapes=scratch,
        compiler_params=pltpu.CompilerParams(
            dimension_semantics=("arbitrary",), vmem_limit_bytes=GRANT
        ),
        cost_estimate=pl.CostEstimate(flops=flops, bytes_accessed=moved, transcendentals=exps),
    )


def array(shape, dtype):
    return jax.ShapeDtypeStruct(shape, dtype)


def make_calls(crops, protos, size, dps, parts):
    steps = protos // BLOCK
    lines, tiles = crops // LANES, protos // LANES
    across = pl.BlockSpec((crops, BLOCK), lambda step: (0, step))
    down = pl.BlockSpec((BLOCK, size), lambda step: (step, 0))
    matrix = crops * protos
    product = 2 * matrix * size
    col_sent = (array((dps, tiles, LANES), BF16), whole((dps, tiles, LANES)))
    row_sent = (array((parts, lines, LANES), F32), whole((parts, lines, LANES)))
    tall = pltpu.VMEM((crops, LANES), F32)
    short = pltpu.VMEM((tiles, LANES), F32)
    energy = called(
        energy_kernel, steps, [whole((crops, size)), down],
        [(array((crops, protos), BF16), across), col_sent],
        [short], product, 2 * matrix, matrix,
    )
    rows = called(
        row_kernel, steps, [whole((dps, tiles, LANES)), across], [row_sent], [short, tall], 2 * matrix, 2 * matrix
    )
    cols = called(
        col_kernel, steps, [whole((parts, lines, LANES)), across], [col_sent], [tall, short], 2 * matrix, 2 * matrix
    )
    student = called(
        student_kernel, steps, [whole((crops, size)), down],
        [
            (array((crops, protos), BF16), across),
            (array((crops, size), F32), whole((crops, size))),
            (array((lines, LANES), F32), whole((lines, LANES))),
        ],
        [tall], 2 * product, 2 * matrix, matrix,
    )
    last = called(
        last_kernel, steps,
        [whole((dps, tiles, LANES)), whole((lines, LANES)), across, whole((crops, size)), down],
        [
            (array((parts, 3 * lines, LANES), F32), whole((parts, 3 * lines, LANES))),
            (array((crops, size), F32), whole((crops, size))),
            (array((tiles, LANES), F32), whole((tiles, LANES))),
        ],
        [tall, pltpu.VMEM((crops, BLOCK), BF16)], product, 2 * matrix,
    )
    unit_grad = called(
        unit_grad_kernel, 1,
        [whole((parts, 3 * lines, LANES)), whole((crops, size)), whole((crops, size))],
        [
            (array((crops, size), BF16), whole((crops, size))),
            (array((lines, LANES), F32), whole((lines, LANES))),
            (array((crops, LANES), F32), whole((crops, LANES))),
            (array((crops, LANES), F32), whole((crops, LANES))),
        ],
        [], 4 * crops * size, 10 * crops * size,
    )
    wide = protos // dps
    one = pl.BlockSpec((crops, wide), lambda step, core: (0, 2 * step + core[0]))
    proto_grad = pl.pallas_call(
        proto_grad_kernel,
        grid_spec=pltpu.PrefetchScalarGridSpec(
            num_scalar_prefetch=1,
            grid=(dps // 2,),
            in_specs=[
                pl.BlockSpec((size, crops), lambda step, core: (0, 0)),
                pl.BlockSpec((crops, LANES), lambda step, core: (0, 0)),
                pl.BlockSpec((crops, LANES), lambda step, core: (0, 0)),
                pl.BlockSpec((tiles, LANES), lambda step, core: (0, 0)),
                one,
                one,
            ],
            out_specs=pl.BlockSpec((1, size, wide), lambda step, core: (step, 0, 0)),
        ),
        out_shape=array((dps // 2, size, wide), BF16),
        compiler_params=pltpu.CompilerParams(dimension_semantics=("arbitrary",), vmem_limit_bytes=GRANT),
        cost_estimate=pl.CostEstimate(flops=product // 2, bytes_accessed=2 * matrix + protos * size, transcendentals=0),
    )
    return energy, rows, cols, student, last, unit_grad, proto_grad


def summed_protos(keep, give):
    me = lax.axis_index("dp")
    along_y, along_x = (me // 2) % 4, me // 8
    blocks = (keep.astype(F32) + swapped(give, "dp", 1).astype(F32)).astype(BF16)
    blocks = yield blocks.reshape((2, 4) + keep.shape[1:])
    total = lax.dynamic_index_in_dim(blocks, along_y, 1, False).astype(F32)
    for step in range(1, 4):
        give = lax.dynamic_index_in_dim(blocks, (along_y + step) % 4, 1, False)
        pairs = [(one, (one & 9) | ((one + 2 * step) & 6)) for one in range(16)]
        total = total + lax.ppermute(give, "dp", pairs).astype(F32)
    blocks = yield total.astype(BF16)
    keep = lax.dynamic_index_in_dim(blocks, along_x, 0, False)
    give = lax.dynamic_index_in_dim(blocks, 1 - along_x, 0, False)
    yield keep.astype(F32) + swapped(give, "dp", 8).astype(F32)


def body(
    student_cls,
    teacher_cls,
    student_gain,
    teacher_gain,
    student_proj,
    teacher_proj,
    prototypes,
    partner,
):
    crops, width = student_cls.shape
    parts = lax.axis_size("proto")
    own = crops // parts
    size = student_proj.shape[1]
    start = lax.axis_index("proto") * width
    opposite = swapped(student_cls, "dp", 8)
    gain_s = lax.dynamic_slice_in_dim(student_gain, start, width)
    gain_t = lax.dynamic_slice_in_dim(teacher_gain, start, width)

    teacher_blocks = packed_shares(teacher_cls, gain_t, teacher_proj, parts)
    teacher_hidden = summed_hidden(exchanged(teacher_blocks, "proto"))
    teacher_unit = unit_rows(teacher_hidden)[0].astype(BF16)
    teacher_all = from_all(teacher_unit, "proto").reshape(crops, size)

    pick = partner[:, None] % crops == jnp.arange(crops, dtype=jnp.int32)[None]
    turned = lax.dot_general(
        opposite, pick.astype(BF16), (((0,), (1,)), ((), ())), preferred_element_type=F32
    ).astype(BF16)
    weight = (gain_s[:, None] * student_proj.astype(F32)).astype(BF16)
    gathered = lax.all_gather(jnp.concatenate([turned, weight], 1), "proto", axis=0, tiled=True)

    proto_unit32, proto_factor = unit_rows(prototypes.astype(F32))
    proto_unit = proto_unit32.astype(BF16)
    protos = proto_unit.shape[0]
    energy_call, row_call, col_call, student_call, last_call, unit_grad_call, proto_grad_call = make_calls(
        crops, protos, size, lax.axis_size("dp"), parts
    )
    energy, sums = energy_call(teacher_all, proto_unit)
    for step in range(ITERS - 1):
        (sums,) = row_call(exchanged(sums, "dp"), energy)
        (sums,) = col_call(exchanged(sums, "proto"), energy)

    values = gathered[:, :crops].astype(F32)
    student_center, student_scale = center_and_scale(
        jnp.sum(values, axis=0)[:, None], jnp.sum(values * values, axis=0)[:, None]
    )
    weight = gathered[:, crops:]
    student_hidden = student_scale * (
        contract_first(gathered[:, :crops], weight) - student_center * jnp.sum(weight.astype(F32), axis=0)[None]
    )
    student_unit32, student_factor = unit_rows(student_hidden)
    student_unit = student_unit32.astype(BF16)
    sums, student_unit = lax.optimization_barrier((sums, student_unit))
    exponent, pulled, partition = student_call(student_unit, proto_unit)
    sums = exchanged(sums, "dp")
    sums, exponent, pulled, partition = lax.optimization_barrier((sums, exponent, pulled, partition))
    sums, coded, scale = last_call(sums, partition, energy, student_unit, proto_unit)
    unit_grad, crop_loss, wanted, given = unit_grad_call(exchanged(sums, "proto"), pulled, coded)
    core = (lax.axis_index("dp") % 2).reshape(1)
    details = (student_unit.T, wanted, given, scale, exponent, energy)
    give = proto_grad_call(1 - core, *details)
    give, unit_grad = lax.optimization_barrier((give, unit_grad))
    unit_grad = exchanged(unit_grad.reshape(parts, own, size), "proto")
    stages = summed_protos(proto_grad_call(core, *details), give)
    blocks = next(stages)
    crop_loss = swapped(crop_loss, "dp", 8).reshape(1, crops)
    crop_loss = jnp.sum(jnp.where(pick, crop_loss, 0.0), axis=1)
    student_unit32, student_factor, student_center, student_scale = (
        lax.dynamic_slice_in_dim(value, lax.axis_index("proto") * own, own, 0)
        for value in (student_unit32, student_factor, student_center, student_scale)
    )
    unit_grad = jnp.sum(unit_grad.astype(F32), axis=0)
    hidden_grad = student_factor * (
        unit_grad - student_unit32 * jnp.sum(student_unit32 * unit_grad, axis=1, keepdims=True)
    )
    sent = (hidden_grad * student_scale).astype(BF16)
    moved = jnp.stack(three_terms(jnp.sum(student_center * sent.astype(F32), axis=0)))
    packed = jnp.concatenate([sent, moved], 0)
    packed, blocks = lax.optimization_barrier((packed, blocks))
    blocks = stages.send(blocks)
    packed = from_all(packed, "proto")
    moved = jnp.sum(packed[:, own:].astype(F32), axis=(0, 1))
    sent = packed[:, :own].reshape(crops, size)
    share = (gain_s[:, None] * (jnp.dot(turned, sent, preferred_element_type=F32) - moved[None])).astype(BF16)
    share, blocks = lax.optimization_barrier((share, blocks))
    near = [[8 * x + other for other in range(8)] for x in range(2)]
    share = lax.all_to_all(jnp.broadcast_to(share[None], (8,) + share.shape), "dp", 0, 0, axis_index_groups=near)
    share = jnp.sum(share.astype(F32), axis=0).astype(BF16)
    proto_unit_grad = stages.send(blocks).T
    grad_proj = share.astype(F32) + swapped(share, "dp", 8).astype(F32)

    count = protos // lax.axis_size("dp")
    own_start = lax.axis_index("dp") * count
    own_unit, own_factor = unit_rows(
        lax.dynamic_slice_in_dim(prototypes, own_start, count, 0).astype(F32)
    )
    grad_protos = own_factor * (
        proto_unit_grad - own_unit * jnp.sum(own_unit * proto_unit_grad, axis=1, keepdims=True)
    )
    teacher_next = MOMENTUM * teacher_proj + (1.0 - MOMENTUM) * student_proj.astype(F32)
    return (crop_loss, grad_proj, grad_protos, teacher_next)


def solution(mesh):
    placed = (
        P("dp", "proto"),
        P("dp", "proto"),
        P(),
        P(),
        P("proto", None),
        P("proto", None),
        P("proto", None),
        P("dp"),
    )
    return jax.shard_map(
        body,
        mesh=mesh,
        in_specs=placed,
        out_specs=(P("dp"), P("proto", None), P(("proto", "dp"), None), P("proto", None)),
        check_vma=False,
    )
```

```python
import jax
import jax.numpy as jnp
from jax import lax
from jax.experimental import pallas as pl
from jax.experimental.pallas import tpu as pltpu
from jax.sharding import PartitionSpec as P

D = 1536
ITERS = 3


EPSILON = 1e-06
TEACHER_TEMP = 0.07
STUDENT_TEMP = 0.1
MOMENTUM = 0.994
BF16 = jnp.bfloat16
F32 = jnp.float32
LOG2E = 1.4426950408889634
BLOCK = 1024
GRANT = 56 * 1024 * 1024
LANES = 128


def contract_last(left, right):
    return lax.dot_general(left, right, (((1,), (1,)), ((), ())), preferred_element_type=F32)


def contract_first(left, right):
    return lax.dot_general(left, right, (((0,), (0,)), ((), ())), preferred_element_type=F32)


def unit_rows(values):
    factor = lax.rsqrt(jnp.sum(values * values, axis=1, keepdims=True) + EPSILON)
    return (values * factor, factor)


def exchanged(blocks, axis):
    return lax.all_to_all(blocks, axis, 0, 0)


def from_all(value, axis):
    count = lax.axis_size(axis)
    return exchanged(jnp.broadcast_to(value[None], (count,) + value.shape), axis)


def three_terms(value):
    high = value.astype(BF16)
    rest = value - high.astype(F32)
    middle = rest.astype(BF16)
    low = (rest - middle.astype(F32)).astype(BF16)
    return high, middle, low


def swapped(value, axis, bit):
    count = lax.axis_size(axis)
    return lax.ppermute(value, axis, [(one, one ^ bit) for one in range(count)])


def partial_hidden(features, gain, weight):
    scaled = (gain[:, None] * weight.astype(BF16).astype(F32)).astype(BF16)
    share = jnp.dot(features, scaled, preferred_element_type=F32)
    column = jnp.sum(scaled.astype(F32), axis=0)
    values = features.astype(F32)
    return share, column, jnp.sum(values, axis=1), jnp.sum(values * values, axis=1)


def center_and_scale(first, second):
    center = first / D
    return center, lax.rsqrt(second / D - center * center + EPSILON)


def packed_shares(features, gain, weight, parts):
    crops, size = features.shape[0], weight.shape[1]
    own = crops // parts
    share, column, first, second = partial_hidden(features, gain, weight)
    sums = jnp.stack(three_terms(jnp.stack([first, second])))
    sums = sums.reshape(6, parts, own).transpose(1, 0, 2).reshape(parts, 1, 6 * own)
    sums = jnp.pad(sums, ((0, 0), (0, 0), (0, size - 6 * own)))
    columns = jnp.broadcast_to(jnp.stack(three_terms(column))[None], (parts, 3, size))
    return jnp.concatenate([share.astype(BF16).reshape(parts, own, size), columns, sums], 1)


def summed_hidden(packed):
    own = packed.shape[1] - 4
    packed = jnp.sum(packed.astype(F32), axis=0)
    sums = jnp.sum(packed[own + 3, : 6 * own].reshape(3, 2, own), axis=0)
    center, scale = center_and_scale(sums[0][:, None], sums[1][:, None])
    column = jnp.sum(packed[own : own + 3], axis=0)[None]
    return scale * (packed[:own] - center * column)


def column_form(rows):
    return jnp.concatenate(
        [jnp.transpose(jnp.broadcast_to(rows[q : q + 1], (LANES, LANES))) for q in range(rows.shape[0])], 0
    )


def row_form(partial):
    return jnp.concatenate(
        [
            jnp.sum(jnp.transpose(partial[q * LANES : (q + 1) * LANES]), axis=0, keepdims=True)
            for q in range(partial.shape[0] // LANES)
        ],
        0,
    )


def stack_sum(ref):
    total = ref[0].astype(F32)
    for one in range(1, ref.shape[0]):
        total = total + ref[one].astype(F32)
    return total


def energy_kernel(teacher_ref, protos_ref, energy_ref, sums_ref, held):
    step = pl.program_id(0)
    rows = []
    for part in range(BLOCK // 256):
        cut = slice(part * 256, part * 256 + 256)
        value = jnp.exp2(contract_last(teacher_ref[...], protos_ref[cut, :]) * (LOG2E / TEACHER_TEMP))
        energy_ref[:, cut] = value.astype(BF16)
        total = jnp.sum(value, axis=0, keepdims=True)
        rows += [total[:, :LANES], total[:, LANES:]]
    held[pl.ds(pl.multiple_of(step * 8, 8), 8), :] = jnp.concatenate(rows, 0)

    @pl.when(step == pl.num_programs(0) - 1)
    def _():
        for one in range(sums_ref.shape[0]):
            sums_ref[one] = held[...].astype(BF16)


def row_kernel(got_ref, energy_ref, sums_ref, scale, held):
    step = pl.program_id(0)

    @pl.when(step == 0)
    def _():
        scale[...] = 1.0 / stack_sum(got_ref)
        held[...] = jnp.zeros_like(held)

    start = step * 8
    for low in range(0, held.shape[0], LANES):
        cut = slice(low, low + LANES)
        total = held[cut, :]
        for tile in range(8):
            total = total + energy_ref[cut, tile * LANES : (tile + 1) * LANES].astype(F32) * scale[pl.ds(start + tile, 1), :]
        held[cut, :] = total

    @pl.when(step == pl.num_programs(0) - 1)
    def _():
        total = row_form(held[...])
        for one in range(sums_ref.shape[0]):
            sums_ref[one] = total


def col_kernel(got_ref, energy_ref, sums_ref, scale, held):
    step = pl.program_id(0)

    @pl.when(step == 0)
    def _():
        scale[...] = column_form(1.0 / stack_sum(got_ref))

    rows = []
    for tile in range(8):
        value = energy_ref[:, tile * LANES : (tile + 1) * LANES].astype(F32) * scale[...]
        rows.append(jnp.sum(value, axis=0, keepdims=True))
    held[pl.ds(pl.multiple_of(step * 8, 8), 8), :] = jnp.concatenate(rows, 0)

    @pl.when(step == pl.num_programs(0) - 1)
    def _():
        for one in range(sums_ref.shape[0]):
            sums_ref[one] = held[...].astype(BF16)


def student_kernel(student_ref, protos_ref, exponent_ref, pulled_ref, partition_ref, held):
    step = pl.program_id(0)

    @pl.when(step == 0)
    def _():
        held[...] = jnp.zeros_like(held)
        pulled_ref[...] = jnp.zeros_like(pulled_ref)

    for part in range(BLOCK // 256):
        cut = slice(part * 256, part * 256 + 256)
        value = jnp.exp2(contract_last(student_ref[...], protos_ref[cut, :]) * (LOG2E / STUDENT_TEMP))
        held[...] += value[:, :LANES] + value[:, LANES:]
        exponent_ref[:, cut] = value.astype(BF16)
    pulled_ref[...] += jnp.dot(exponent_ref[...], protos_ref[...], preferred_element_type=F32)

    @pl.when(step == pl.num_programs(0) - 1)
    def _():
        partition_ref[...] = row_form(held[...])


def last_kernel(got_ref, partition_ref, energy_ref, student_ref, protos_ref, sums_ref, coded_ref, scale_ref, held, scaled):
    step = pl.program_id(0)

    @pl.when(step == 0)
    def _():
        scale_ref[...] = 1.0 / stack_sum(got_ref)
        held[...] = jnp.zeros_like(held)
        coded_ref[...] = jnp.zeros_like(coded_ref)

    start = step * 8
    for part in range(BLOCK // 256):
        left = energy_ref[:, part * 256 : part * 256 + LANES].astype(F32) * scale_ref[pl.ds(start + 2 * part, 1), :]
        right = energy_ref[:, part * 256 + LANES : part * 256 + 256].astype(F32) * scale_ref[pl.ds(start + 2 * part + 1, 1), :]
        held[...] += left + right
        scaled[:, part * 256 : part * 256 + LANES] = left.astype(BF16)
        scaled[:, part * 256 + LANES : part * 256 + 256] = right.astype(BF16)
    coded_ref[...] += jnp.dot(scaled[...], protos_ref[...], preferred_element_type=F32)

    @pl.when(step == pl.num_programs(0) - 1)
    def _():
        value = student_ref[...].astype(F32) * coded_ref[...]
        expected = value[:, :LANES]
        for tile in range(1, value.shape[1] // LANES):
            expected = expected + value[:, tile * LANES : (tile + 1) * LANES]
        total = jnp.concatenate(
            [row_form(held[...]), partition_ref[...], row_form(expected) * (1.0 / STUDENT_TEMP)], 0
        )
        for one in range(sums_ref.shape[0]):
            sums_ref[one] = total


def unit_grad_kernel(got_ref, pulled_ref, coded_ref, grad_ref, loss_ref, wanted_ref, given_ref):
    total = stack_sum(got_ref)
    count = total.shape[0] // 3
    row = 1.0 / total[:count]
    partition = total[count : 2 * count]
    loss_ref[...] = jnp.log(partition) - total[2 * count :] * row
    wanted = column_form(1.0 / (partition * STUDENT_TEMP))
    given = column_form(row * (1.0 / STUDENT_TEMP))
    wanted_ref[...] = wanted
    given_ref[...] = given
    for tile in range(pulled_ref.shape[1] // LANES):
        cut = slice(tile * LANES, (tile + 1) * LANES)
        grad_ref[:, cut] = (pulled_ref[:, cut] * wanted - coded_ref[:, cut] * given).astype(BF16)


def proto_grad_kernel(core_ref, turned_ref, wanted_ref, given_ref, scale_ref, exponent_ref, energy_ref, out_ref):
    line = pl.program_id(0) * 4 + core_ref[0] * 2
    parts = []
    for half in range(2):
        cut = slice(half * LANES, half * LANES + LANES)
        scale = scale_ref[pl.ds(line + half, 1), :]
        score = exponent_ref[:, cut].astype(F32) * wanted_ref[...] - energy_ref[:, cut].astype(F32) * scale * given_ref[...]
        parts.append(score.astype(BF16))
    out_ref[0] = jnp.dot(turned_ref[...], jnp.concatenate(parts, 1), preferred_element_type=F32).astype(BF16)


def hidden_grad_kernel(got_ref, unit_ref, factor_ref, out_ref):
    grad = stack_sum(got_ref)
    unit = unit_ref[...]
    grad = factor_ref[...] * (grad - unit * jnp.sum(unit * grad, axis=1, keepdims=True))
    grad = grad.astype(BF16)
    for one in range(out_ref.shape[0]):
        out_ref[one] = grad


def whole(shape):
    return pl.BlockSpec(shape, lambda step: (0,) * len(shape))


def called(kernel, steps, ins, outs, scratch, flops=0, moved=0, exps=0):
    return pl.pallas_call(
        kernel,
        grid=(steps,),
        in_specs=ins,
        out_specs=[spec for _, spec in outs],
        out_shape=[shape for shape, _ in outs],
        scratch_shapes=scratch,
        compiler_params=pltpu.CompilerParams(
            dimension_semantics=("arbitrary",), vmem_limit_bytes=GRANT
        ),
        cost_estimate=pl.CostEstimate(flops=flops, bytes_accessed=moved, transcendentals=exps),
    )


def array(shape, dtype):
    return jax.ShapeDtypeStruct(shape, dtype)


def make_calls(crops, protos, size, dps, parts):
    steps = protos // BLOCK
    lines, tiles = crops // LANES, protos // LANES
    across = pl.BlockSpec((crops, BLOCK), lambda step: (0, step))
    down = pl.BlockSpec((BLOCK, size), lambda step: (step, 0))
    matrix = crops * protos
    product = 2 * matrix * size
    col_sent = (array((dps, tiles, LANES), BF16), whole((dps, tiles, LANES)))
    row_sent = (array((parts, lines, LANES), F32), whole((parts, lines, LANES)))
    tall = pltpu.VMEM((crops, LANES), F32)
    short = pltpu.VMEM((tiles, LANES), F32)
    energy = called(
        energy_kernel, steps, [whole((crops, size)), down],
        [(array((crops, protos), BF16), across), col_sent],
        [short], product, 2 * matrix, matrix,
    )
    rows = called(
        row_kernel, steps, [whole((dps, tiles, LANES)), across], [row_sent], [short, tall], 2 * matrix, 2 * matrix
    )
    cols = called(
        col_kernel, steps, [whole((parts, lines, LANES)), across], [col_sent], [tall, short], 2 * matrix, 2 * matrix
    )
    student = called(
        student_kernel, steps, [whole((crops, size)), down],
        [
            (array((crops, protos), BF16), across),
            (array((crops, size), F32), whole((crops, size))),
            (array((lines, LANES), F32), whole((lines, LANES))),
        ],
        [tall], 2 * product, 2 * matrix, matrix,
    )
    last = called(
        last_kernel, steps,
        [whole((dps, tiles, LANES)), whole((lines, LANES)), across, whole((crops, size)), down],
        [
            (array((parts, 3 * lines, LANES), F32), whole((parts, 3 * lines, LANES))),
            (array((crops, size), F32), whole((crops, size))),
            (array((tiles, LANES), F32), whole((tiles, LANES))),
        ],
        [tall, pltpu.VMEM((crops, BLOCK), BF16)], product, 2 * matrix,
    )
    unit_grad = called(
        unit_grad_kernel, 1,
        [whole((parts, 3 * lines, LANES)), whole((crops, size)), whole((crops, size))],
        [
            (array((crops, size), BF16), whole((crops, size))),
            (array((lines, LANES), F32), whole((lines, LANES))),
            (array((crops, LANES), F32), whole((crops, LANES))),
            (array((crops, LANES), F32), whole((crops, LANES))),
        ],
        [], 4 * crops * size, 10 * crops * size,
    )
    own = crops // parts
    hidden_grad = called(
        hidden_grad_kernel, 1, [whole((parts, own, size)), whole((own, size)), whole((own, 1))],
        [(array((parts, own, size), BF16), whole((parts, own, size)))], [], 6 * own * size, 4 * crops * size,
    )
    wide = protos // dps
    one = pl.BlockSpec((crops, wide), lambda step, core: (0, 2 * step + core[0]))
    proto_grad = pl.pallas_call(
        proto_grad_kernel,
        grid_spec=pltpu.PrefetchScalarGridSpec(
            num_scalar_prefetch=1,
            grid=(dps // 2,),
            in_specs=[
                pl.BlockSpec((size, crops), lambda step, core: (0, 0)),
                pl.BlockSpec((crops, LANES), lambda step, core: (0, 0)),
                pl.BlockSpec((crops, LANES), lambda step, core: (0, 0)),
                pl.BlockSpec((tiles, LANES), lambda step, core: (0, 0)),
                one,
                one,
            ],
            out_specs=pl.BlockSpec((1, size, wide), lambda step, core: (step, 0, 0)),
        ),
        out_shape=array((dps // 2, size, wide), BF16),
        compiler_params=pltpu.CompilerParams(dimension_semantics=("arbitrary",), vmem_limit_bytes=GRANT),
        cost_estimate=pl.CostEstimate(flops=product // 2, bytes_accessed=2 * matrix + protos * size, transcendentals=0),
    )
    return energy, rows, cols, student, last, unit_grad, hidden_grad, proto_grad


def summed_protos(keep, give):
    me = lax.axis_index("dp")
    along_y, along_x = (me // 2) % 4, me // 8
    blocks = (keep.astype(F32) + swapped(give, "dp", 1).astype(F32)).astype(BF16)
    blocks = yield blocks.reshape((2, 4) + keep.shape[1:])
    terms = [lax.dynamic_index_in_dim(blocks, along_y, 1, False)]
    for step in range(1, 4):
        give = lax.dynamic_index_in_dim(blocks, (along_y + step) % 4, 1, False)
        pairs = [(one, (one & 9) | ((one + 2 * step) & 6)) for one in range(16)]
        terms.append(lax.ppermute(give, "dp", pairs))
    terms = yield terms
    blocks = sum(term.astype(F32) for term in terms).astype(BF16)
    keep = lax.dynamic_index_in_dim(blocks, along_x, 0, False)
    give = lax.dynamic_index_in_dim(blocks, 1 - along_x, 0, False)
    yield keep.astype(F32) + swapped(give, "dp", 8).astype(F32)


def body(
    student_cls,
    teacher_cls,
    student_gain,
    teacher_gain,
    student_proj,
    teacher_proj,
    prototypes,
    partner,
):
    crops, width = student_cls.shape
    parts = lax.axis_size("proto")
    own = crops // parts
    size = student_proj.shape[1]
    start = lax.axis_index("proto") * width
    opposite = swapped(student_cls, "dp", 8)
    gain_s = lax.dynamic_slice_in_dim(student_gain, start, width)
    gain_t = lax.dynamic_slice_in_dim(teacher_gain, start, width)

    teacher_blocks = packed_shares(teacher_cls, gain_t, teacher_proj, parts)
    teacher_hidden = summed_hidden(exchanged(teacher_blocks, "proto"))
    teacher_unit = unit_rows(teacher_hidden)[0].astype(BF16)
    teacher_all = from_all(teacher_unit, "proto").reshape(crops, size)

    pick = partner[:, None] % crops == jnp.arange(crops, dtype=jnp.int32)[None]
    turned = lax.dot_general(
        opposite, pick.astype(BF16), (((0,), (1,)), ((), ())), preferred_element_type=F32
    ).astype(BF16)
    weight = (gain_s[:, None] * student_proj.astype(F32)).astype(BF16)
    gathered = lax.all_gather(jnp.concatenate([turned, weight], 1), "proto", axis=0, tiled=True)

    proto_unit32, proto_factor = unit_rows(prototypes.astype(F32))
    proto_unit = proto_unit32.astype(BF16)
    protos = proto_unit.shape[0]
    calls = make_calls(crops, protos, size, lax.axis_size("dp"), parts)
    energy_call, row_call, col_call, student_call, last_call, unit_grad_call, hidden_grad_call, proto_grad_call = calls
    energy, sums = energy_call(teacher_all, proto_unit)
    values = gathered[:, :crops].astype(F32)
    student_center, student_scale = center_and_scale(
        jnp.sum(values, axis=0)[:, None], jnp.sum(values * values, axis=0)[:, None]
    )
    weight = gathered[:, crops:]
    student_hidden = student_scale * (
        contract_first(gathered[:, :crops], weight) - student_center * jnp.sum(weight.astype(F32), axis=0)[None]
    )
    student_unit32, student_factor = unit_rows(student_hidden)
    student_unit = student_unit32.astype(BF16)
    normed = turned.astype(F32) - student_center.reshape(1, crops)
    normed = (normed * student_scale.reshape(1, crops) * gain_s[:, None]).astype(BF16)
    student_unit32, student_factor = (
        lax.dynamic_slice_in_dim(value, lax.axis_index("proto") * own, own, 0)
        for value in (student_unit32, student_factor)
    )
    student = (student_unit, student_unit32, student_factor, normed)
    for step in range(ITERS - 1):
        (sums,) = row_call(exchanged(sums, "dp"), energy)
        sums = exchanged(sums, "proto")
        if step == ITERS - 2:
            sums, student = lax.optimization_barrier((sums, student))
        (sums,) = col_call(sums, energy)
    student_unit, student_unit32, student_factor, normed = student
    sums, student_unit = lax.optimization_barrier((sums, student_unit))
    exponent, pulled, partition = student_call(student_unit, proto_unit)
    sums = exchanged(sums, "dp")
    sums, exponent, pulled, partition = lax.optimization_barrier((sums, exponent, pulled, partition))
    sums, coded, scale = last_call(sums, partition, energy, student_unit, proto_unit)
    unit_grad, crop_loss, wanted, given = unit_grad_call(exchanged(sums, "proto"), pulled, coded)
    core = (lax.axis_index("dp") % 2).reshape(1)
    details = (student_unit.T, wanted, given, scale, exponent, energy)
    give = proto_grad_call(1 - core, *details)
    give, unit_grad = lax.optimization_barrier((give, unit_grad))
    unit_grad = exchanged(unit_grad.reshape(parts, own, size), "proto")
    stages = summed_protos(proto_grad_call(core, *details), give)
    blocks = next(stages)
    crop_loss = swapped(crop_loss, "dp", 8).reshape(1, crops)
    crop_loss = jnp.sum(jnp.where(pick, crop_loss, 0.0), axis=1)
    unit_grad, blocks = lax.optimization_barrier((unit_grad, blocks))
    (sent,) = hidden_grad_call(unit_grad, student_unit32, student_factor)
    blocks = stages.send(blocks)
    sent = exchanged(sent, "proto").reshape(crops, size)
    share = jnp.dot(normed, sent, preferred_element_type=F32).astype(BF16)
    near = [[8 * x + other for other in range(8)] for x in range(2)]
    share = lax.all_to_all(jnp.broadcast_to(share[None], (8,) + share.shape), "dp", 0, 0, axis_index_groups=near)
    share, blocks = lax.optimization_barrier((share, blocks))
    blocks = stages.send(blocks)
    share = jnp.sum(share.astype(F32), axis=0).astype(BF16)
    proto_unit_grad = blocks.T
    grad_proj = share.astype(F32) + swapped(share, "dp", 8).astype(F32)

    count = protos // lax.axis_size("dp")
    own_start = lax.axis_index("dp") * count
    own_unit, own_factor = unit_rows(
        lax.dynamic_slice_in_dim(prototypes, own_start, count, 0).astype(F32)
    )
    grad_protos = own_factor * (
        proto_unit_grad - own_unit * jnp.sum(own_unit * proto_unit_grad, axis=1, keepdims=True)
    )
    teacher_next = MOMENTUM * teacher_proj + (1.0 - MOMENTUM) * student_proj.astype(F32)
    return (crop_loss, grad_proj, grad_protos, teacher_next)


def solution(mesh):
    placed = (
        P("dp", "proto"),
        P("dp", "proto"),
        P(),
        P(),
        P("proto", None),
        P("proto", None),
        P("proto", None),
        P("dp"),
    )
    return jax.shard_map(
        body,
        mesh=mesh,
        in_specs=placed,
        out_specs=(P("dp"), P("proto", None), P(("proto", "dp"), None), P("proto", None)),
        check_vma=False,
    )
```

```python
import jax
import jax.numpy as jnp
from jax import lax
from jax.experimental import pallas as pl
from jax.experimental.pallas import tpu as pltpu
from jax.sharding import PartitionSpec as P

D = 1536
ITERS = 3


EPSILON = 1e-06
TEACHER_TEMP = 0.07
STUDENT_TEMP = 0.1
MOMENTUM = 0.994
BF16 = jnp.bfloat16
F32 = jnp.float32
LOG2E = 1.4426950408889634
BLOCK = 1024
GRANT = 16 * 1024 * 1024
LANES = 128


def contract_last(left, right):
    return lax.dot_general(left, right, (((1,), (1,)), ((), ())), preferred_element_type=F32)


def contract_first(left, right):
    return lax.dot_general(left, right, (((0,), (0,)), ((), ())), preferred_element_type=F32)


def unit_rows(values):
    factor = lax.rsqrt(jnp.sum(values * values, axis=1, keepdims=True) + EPSILON)
    return (values * factor, factor)


def exchanged(blocks, axis):
    return lax.all_to_all(blocks, axis, 0, 0)


def from_all(value, axis):
    count = lax.axis_size(axis)
    return exchanged(jnp.broadcast_to(value[None], (count,) + value.shape), axis)


def three_terms(value):
    high = value.astype(BF16)
    rest = value - high.astype(F32)
    middle = rest.astype(BF16)
    low = (rest - middle.astype(F32)).astype(BF16)
    return high, middle, low


def swapped(value, axis, bit):
    count = lax.axis_size(axis)
    return lax.ppermute(value, axis, [(one, one ^ bit) for one in range(count)])


def partial_hidden(features, gain, weight):
    scaled = (gain[:, None] * weight.astype(BF16).astype(F32)).astype(BF16)
    share = jnp.dot(features, scaled, preferred_element_type=F32)
    column = jnp.sum(scaled.astype(F32), axis=0)
    values = features.astype(F32)
    return share, column, jnp.sum(values, axis=1), jnp.sum(values * values, axis=1)


def center_and_scale(first, second):
    center = first / D
    return center, lax.rsqrt(second / D - center * center + EPSILON)


def packed_shares(features, gain, weight, parts):
    crops, size = features.shape[0], weight.shape[1]
    own = crops // parts
    share, column, first, second = partial_hidden(features, gain, weight)
    sums = jnp.stack(three_terms(jnp.stack([first, second])))
    sums = sums.reshape(6, parts, own).transpose(1, 0, 2).reshape(parts, 1, 6 * own)
    sums = jnp.pad(sums, ((0, 0), (0, 0), (0, size - 6 * own)))
    columns = jnp.broadcast_to(jnp.stack(three_terms(column))[None], (parts, 3, size))
    return jnp.concatenate([share.astype(BF16).reshape(parts, own, size), columns, sums], 1)


def summed_hidden(packed):
    own = packed.shape[1] - 4
    packed = jnp.sum(packed.astype(F32), axis=0)
    sums = jnp.sum(packed[own + 3, : 6 * own].reshape(3, 2, own), axis=0)
    center, scale = center_and_scale(sums[0][:, None], sums[1][:, None])
    column = jnp.sum(packed[own : own + 3], axis=0)[None]
    return scale * (packed[:own] - center * column)


def column_form(rows):
    return jnp.concatenate(
        [jnp.transpose(jnp.broadcast_to(rows[q : q + 1], (LANES, LANES))) for q in range(rows.shape[0])], 0
    )


def row_form(partial):
    return jnp.concatenate(
        [
            jnp.sum(jnp.transpose(partial[q * LANES : (q + 1) * LANES]), axis=0, keepdims=True)
            for q in range(partial.shape[0] // LANES)
        ],
        0,
    )


def stack_sum(ref):
    total = ref[0].astype(F32)
    for one in range(1, ref.shape[0]):
        total = total + ref[one].astype(F32)
    return total


def energy_kernel(teacher_ref, protos_ref, energy_ref, sums_ref, held):
    step = pl.program_id(0)
    rows = []
    for part in range(BLOCK // 256):
        cut = slice(part * 256, part * 256 + 256)
        value = jnp.exp2(contract_last(teacher_ref[...], protos_ref[cut, :]) * (LOG2E / TEACHER_TEMP))
        energy_ref[:, cut] = value.astype(BF16)
        total = jnp.sum(value, axis=0, keepdims=True)
        rows += [total[:, :LANES], total[:, LANES:]]
    held[pl.ds(pl.multiple_of(step * 8, 8), 8), :] = jnp.concatenate(rows, 0)

    @pl.when(step == pl.num_programs(0) - 1)
    def _():
        for one in range(sums_ref.shape[0]):
            sums_ref[one] = held[...].astype(BF16)


def row_kernel(got_ref, energy_ref, sums_ref, scale, held):
    step = pl.program_id(0)

    @pl.when(step == 0)
    def _():
        scale[...] = 1.0 / stack_sum(got_ref)
        held[...] = jnp.zeros_like(held)

    start = step * 8
    for low in range(0, held.shape[0], LANES):
        cut = slice(low, low + LANES)
        total = held[cut, :]
        for tile in range(8):
            total = total + energy_ref[cut, tile * LANES : (tile + 1) * LANES].astype(F32) * scale[pl.ds(start + tile, 1), :]
        held[cut, :] = total

    @pl.when(step == pl.num_programs(0) - 1)
    def _():
        total = row_form(held[...])
        for one in range(sums_ref.shape[0]):
            sums_ref[one] = total


def col_kernel(got_ref, energy_ref, sums_ref, scale, held):
    step = pl.program_id(0)

    @pl.when(step == 0)
    def _():
        scale[...] = column_form(1.0 / stack_sum(got_ref))

    rows = []
    for tile in range(8):
        value = energy_ref[:, tile * LANES : (tile + 1) * LANES].astype(F32) * scale[...]
        rows.append(jnp.sum(value, axis=0, keepdims=True))
    held[pl.ds(pl.multiple_of(step * 8, 8), 8), :] = jnp.concatenate(rows, 0)

    @pl.when(step == pl.num_programs(0) - 1)
    def _():
        for one in range(sums_ref.shape[0]):
            sums_ref[one] = held[...].astype(BF16)


def student_kernel(student_ref, protos_ref, exponent_ref, pulled_ref, partition_ref, held):
    step = pl.program_id(0)

    @pl.when(step == 0)
    def _():
        held[...] = jnp.zeros_like(held)
        pulled_ref[...] = jnp.zeros_like(pulled_ref)

    for part in range(BLOCK // 256):
        cut = slice(part * 256, part * 256 + 256)
        value = jnp.exp2(contract_last(student_ref[...], protos_ref[cut, :]) * (LOG2E / STUDENT_TEMP))
        held[...] += value[:, :LANES] + value[:, LANES:]
        exponent_ref[:, cut] = value.astype(BF16)
    pulled_ref[...] += jnp.dot(exponent_ref[...], protos_ref[...], preferred_element_type=F32)

    @pl.when(step == pl.num_programs(0) - 1)
    def _():
        partition_ref[...] = row_form(held[...])


def last_kernel(got_ref, partition_ref, energy_ref, student_ref, protos_ref, sums_ref, coded_ref, scale_ref, held, scaled):
    step = pl.program_id(0)

    @pl.when(step == 0)
    def _():
        scale_ref[...] = 1.0 / stack_sum(got_ref)
        held[...] = jnp.zeros_like(held)
        coded_ref[...] = jnp.zeros_like(coded_ref)

    start = step * 8
    for part in range(BLOCK // 256):
        left = energy_ref[:, part * 256 : part * 256 + LANES].astype(F32) * scale_ref[pl.ds(start + 2 * part, 1), :]
        right = energy_ref[:, part * 256 + LANES : part * 256 + 256].astype(F32) * scale_ref[pl.ds(start + 2 * part + 1, 1), :]
        held[...] += left + right
        scaled[:, part * 256 : part * 256 + LANES] = left.astype(BF16)
        scaled[:, part * 256 + LANES : part * 256 + 256] = right.astype(BF16)
    coded_ref[...] += jnp.dot(scaled[...], protos_ref[...], preferred_element_type=F32)

    @pl.when(step == pl.num_programs(0) - 1)
    def _():
        value = student_ref[...].astype(F32) * coded_ref[...]
        expected = value[:, :LANES]
        for tile in range(1, value.shape[1] // LANES):
            expected = expected + value[:, tile * LANES : (tile + 1) * LANES]
        total = jnp.concatenate(
            [row_form(held[...]), partition_ref[...], row_form(expected) * (1.0 / STUDENT_TEMP)], 0
        )
        for one in range(sums_ref.shape[0]):
            sums_ref[one] = total


def proto_block(line, turned_ref, wanted_ref, given_ref, scale_ref, exponent_ref, energy_ref, out_ref):
    parts = []
    for half in range(2):
        cut = slice(half * LANES, half * LANES + LANES)
        scale = scale_ref[pl.ds(line + half, 1), :]
        score = exponent_ref[:, cut].astype(F32) * wanted_ref[...] - energy_ref[:, cut].astype(F32) * scale * given_ref[...]
        parts.append(score.astype(BF16))
    out_ref[0] = jnp.dot(turned_ref[...], jnp.concatenate(parts, 1), preferred_element_type=F32).astype(BF16)


def unit_grad_kernel(
    core_ref, got_ref, pulled_ref, coded_ref, turned_ref, scale_ref, exponent_ref, energy_ref,
    grad_ref, loss_ref, wanted_ref, given_ref, out_ref,
):
    @pl.when(pl.program_id(0) == 0)
    def _():
        total = stack_sum(got_ref)
        count = total.shape[0] // 3
        row = 1.0 / total[:count]
        partition = total[count : 2 * count]
        loss_ref[...] = jnp.log(partition) - total[2 * count :] * row
        wanted = column_form(1.0 / (partition * STUDENT_TEMP))
        given = column_form(row * (1.0 / STUDENT_TEMP))
        wanted_ref[...] = wanted
        given_ref[...] = given
        for tile in range(pulled_ref.shape[1] // LANES):
            cut = slice(tile * LANES, (tile + 1) * LANES)
            grad_ref[:, cut] = (pulled_ref[:, cut] * wanted - coded_ref[:, cut] * given).astype(BF16)

    line = pl.program_id(0) * 4 + core_ref[0] * 2
    proto_block(line, turned_ref, wanted_ref, given_ref, scale_ref, exponent_ref, energy_ref, out_ref)


def proto_grad_kernel(core_ref, turned_ref, wanted_ref, given_ref, scale_ref, exponent_ref, energy_ref, out_ref):
    line = pl.program_id(0) * 4 + core_ref[0] * 2
    proto_block(line, turned_ref, wanted_ref, given_ref, scale_ref, exponent_ref, energy_ref, out_ref)


def hidden_grad_kernel(got_ref, unit_ref, factor_ref, out_ref):
    grad = stack_sum(got_ref)
    unit = unit_ref[...]
    grad = factor_ref[...] * (grad - unit * jnp.sum(unit * grad, axis=1, keepdims=True))
    grad = grad.astype(BF16)
    for one in range(out_ref.shape[0]):
        out_ref[one] = grad


def whole(shape):
    return pl.BlockSpec(shape, lambda step: (0,) * len(shape))


def called(kernel, steps, ins, outs, scratch, flops=0, moved=0, exps=0):
    return pl.pallas_call(
        kernel,
        grid=(steps,),
        in_specs=ins,
        out_specs=[spec for _, spec in outs],
        out_shape=[shape for shape, _ in outs],
        scratch_shapes=scratch,
        compiler_params=pltpu.CompilerParams(
            dimension_semantics=("arbitrary",), vmem_limit_bytes=GRANT
        ),
        cost_estimate=pl.CostEstimate(flops=flops, bytes_accessed=moved, transcendentals=exps),
    )


def array(shape, dtype):
    return jax.ShapeDtypeStruct(shape, dtype)


def make_calls(crops, protos, size, dps, parts):
    steps = protos // BLOCK
    lines, tiles = crops // LANES, protos // LANES
    across = pl.BlockSpec((crops, BLOCK), lambda step: (0, step))
    down = pl.BlockSpec((BLOCK, size), lambda step: (step, 0))
    matrix = crops * protos
    product = 2 * matrix * size
    col_sent = (array((dps, tiles, LANES), BF16), whole((dps, tiles, LANES)))
    row_sent = (array((parts, lines, LANES), F32), whole((parts, lines, LANES)))
    tall = pltpu.VMEM((crops, LANES), F32)
    short = pltpu.VMEM((tiles, LANES), F32)
    energy = called(
        energy_kernel, steps, [whole((crops, size)), down],
        [(array((crops, protos), BF16), across), col_sent],
        [short], product, 2 * matrix, matrix,
    )
    rows = called(
        row_kernel, steps, [whole((dps, tiles, LANES)), across], [row_sent], [short, tall], 2 * matrix, 2 * matrix
    )
    cols = called(
        col_kernel, steps, [whole((parts, lines, LANES)), across], [col_sent], [tall, short], 2 * matrix, 2 * matrix
    )
    student = called(
        student_kernel, steps, [whole((crops, size)), down],
        [
            (array((crops, protos), BF16), across),
            (array((crops, size), F32), whole((crops, size))),
            (array((lines, LANES), F32), whole((lines, LANES))),
        ],
        [tall], 2 * product, 2 * matrix, matrix,
    )
    last = called(
        last_kernel, steps,
        [whole((dps, tiles, LANES)), whole((lines, LANES)), across, whole((crops, size)), down],
        [
            (array((parts, 3 * lines, LANES), F32), whole((parts, 3 * lines, LANES))),
            (array((crops, size), F32), whole((crops, size))),
            (array((tiles, LANES), F32), whole((tiles, LANES))),
        ],
        [tall, pltpu.VMEM((crops, BLOCK), BF16)], product, 2 * matrix,
    )
    own = crops // parts
    hidden_grad = called(
        hidden_grad_kernel, 1, [whole((parts, own, size)), whole((own, size)), whole((own, 1))],
        [(array((parts, own, size), BF16), whole((parts, own, size)))], [], 6 * own * size, 4 * crops * size,
    )
    wide = protos // dps
    one = pl.BlockSpec((crops, wide), lambda step, core: (0, 2 * step + core[0]))
    out = pl.BlockSpec((1, size, wide), lambda step, core: (step, 0, 0))
    params = pltpu.CompilerParams(dimension_semantics=("arbitrary",), vmem_limit_bytes=GRANT)
    cost = pl.CostEstimate(flops=product // 2, bytes_accessed=2 * matrix + protos * size, transcendentals=0)

    def fixed(shape):
        return pl.BlockSpec(shape, lambda step, core: (0,) * len(shape))

    proto_grad = pl.pallas_call(
        proto_grad_kernel,
        grid_spec=pltpu.PrefetchScalarGridSpec(
            num_scalar_prefetch=1,
            grid=(dps // 2,),
            in_specs=[fixed((size, crops)), fixed((crops, LANES)), fixed((crops, LANES)), fixed((tiles, LANES)), one, one],
            out_specs=out,
        ),
        out_shape=array((dps // 2, size, wide), BF16),
        compiler_params=params,
        cost_estimate=cost,
    )
    unit_grad = pl.pallas_call(
        unit_grad_kernel,
        grid_spec=pltpu.PrefetchScalarGridSpec(
            num_scalar_prefetch=1,
            grid=(dps // 2,),
            in_specs=[
                fixed((parts, 3 * lines, LANES)), fixed((crops, size)), fixed((crops, size)),
                fixed((size, crops)), fixed((tiles, LANES)), one, one,
            ],
            out_specs=[fixed((crops, size)), fixed((lines, LANES)), fixed((crops, LANES)), fixed((crops, LANES)), out],
        ),
        out_shape=[
            array((crops, size), BF16), array((lines, LANES), F32), array((crops, LANES), F32),
            array((crops, LANES), F32), array((dps // 2, size, wide), BF16),
        ],
        compiler_params=params,
        cost_estimate=cost,
    )
    return energy, rows, cols, student, last, unit_grad, hidden_grad, proto_grad


def summed_protos(keep, give):
    me = lax.axis_index("dp")
    along_y, along_x = (me // 2) % 4, me // 8
    blocks = (keep.astype(F32) + swapped(give, "dp", 1).astype(F32)).astype(BF16)
    blocks = yield blocks.reshape((2, 4) + keep.shape[1:])
    terms = [lax.dynamic_index_in_dim(blocks, along_y, 1, False)]
    for step in range(1, 4):
        give = lax.dynamic_index_in_dim(blocks, (along_y + step) % 4, 1, False)
        pairs = [(one, (one & 9) | ((one + 2 * step) & 6)) for one in range(16)]
        terms.append(lax.ppermute(give, "dp", pairs))
    terms = yield terms
    blocks = sum(term.astype(F32) for term in terms).astype(BF16)
    keep = lax.dynamic_index_in_dim(blocks, along_x, 0, False)
    give = lax.dynamic_index_in_dim(blocks, 1 - along_x, 0, False)
    yield keep.astype(F32) + swapped(give, "dp", 8).astype(F32)


def body(
    student_cls,
    teacher_cls,
    student_gain,
    teacher_gain,
    student_proj,
    teacher_proj,
    prototypes,
    partner,
):
    crops, width = student_cls.shape
    parts = lax.axis_size("proto")
    own = crops // parts
    size = student_proj.shape[1]
    start = lax.axis_index("proto") * width
    opposite = swapped(student_cls, "dp", 8)
    gain_s = lax.dynamic_slice_in_dim(student_gain, start, width)
    gain_t = lax.dynamic_slice_in_dim(teacher_gain, start, width)

    teacher_blocks = packed_shares(teacher_cls, gain_t, teacher_proj, parts)
    teacher_hidden = summed_hidden(exchanged(teacher_blocks, "proto"))
    teacher_unit = unit_rows(teacher_hidden)[0].astype(BF16)
    teacher_all = from_all(teacher_unit, "proto").reshape(crops, size)

    pick = partner[:, None] % crops == jnp.arange(crops, dtype=jnp.int32)[None]
    turned = lax.dot_general(
        opposite, pick.astype(BF16), (((0,), (1,)), ((), ())), preferred_element_type=F32
    ).astype(BF16)
    weight = (gain_s[:, None] * student_proj.astype(F32)).astype(BF16)
    gathered = lax.all_gather(jnp.concatenate([turned, weight], 1), "proto", axis=0, tiled=True)

    proto_unit32, proto_factor = unit_rows(prototypes.astype(F32))
    proto_unit = proto_unit32.astype(BF16)
    protos = proto_unit.shape[0]
    calls = make_calls(crops, protos, size, lax.axis_size("dp"), parts)
    energy_call, row_call, col_call, student_call, last_call, unit_grad_call, hidden_grad_call, proto_grad_call = calls
    energy, sums = energy_call(teacher_all, proto_unit)
    values = gathered[:, :crops].astype(F32)
    student_center, student_scale = center_and_scale(
        jnp.sum(values, axis=0)[:, None], jnp.sum(values * values, axis=0)[:, None]
    )
    weight = gathered[:, crops:]
    student_hidden = student_scale * (
        contract_first(gathered[:, :crops], weight) - student_center * jnp.sum(weight.astype(F32), axis=0)[None]
    )
    student_unit32, student_factor = unit_rows(student_hidden)
    student_unit = student_unit32.astype(BF16)
    normed = turned.astype(F32) - student_center.reshape(1, crops)
    normed = (normed * student_scale.reshape(1, crops) * gain_s[:, None]).astype(BF16)
    student_unit32, student_factor = (
        lax.dynamic_slice_in_dim(value, lax.axis_index("proto") * own, own, 0)
        for value in (student_unit32, student_factor)
    )
    student = (student_unit, student_unit32, student_factor, normed, student_unit.T)
    for step in range(ITERS - 1):
        sums = exchanged(sums, "dp")
        if step == ITERS - 2:
            sums, student = lax.optimization_barrier((sums, student))
            student_unit, student_unit32, student_factor, normed, turned_unit = student
        (sums,) = row_call(sums, energy)
        if step == ITERS - 2:
            sums, student_unit = lax.optimization_barrier((sums, student_unit))
            fields = student_call(student_unit, proto_unit)
        sums = exchanged(sums, "proto")
        if step == ITERS - 2:
            sums, fields = lax.optimization_barrier((sums, fields))
        (sums,) = col_call(sums, energy)
    exponent, pulled, partition = fields
    sums = exchanged(sums, "dp")
    sums, coded, scale = last_call(sums, partition, energy, student_unit, proto_unit)
    core = (lax.axis_index("dp") % 2).reshape(1)
    unit_grad, crop_loss, wanted, given, give = unit_grad_call(
        1 - core, exchanged(sums, "proto"), pulled, coded, turned_unit, scale, exponent, energy
    )
    unit_grad = exchanged(unit_grad.reshape(parts, own, size), "proto")
    stages = summed_protos(proto_grad_call(core, turned_unit, wanted, given, scale, exponent, energy), give)
    blocks = next(stages)
    crop_loss = swapped(crop_loss, "dp", 8).reshape(1, crops)
    crop_loss = jnp.sum(jnp.where(pick, crop_loss, 0.0), axis=1)
    (sent,) = hidden_grad_call(unit_grad, student_unit32, student_factor)
    sent, blocks = lax.optimization_barrier((sent, blocks))
    blocks = stages.send(blocks)
    sent = exchanged(sent, "proto").reshape(crops, size)
    share = jnp.dot(normed, sent, preferred_element_type=F32).astype(BF16)
    share, blocks = lax.optimization_barrier((share, blocks))
    blocks = stages.send(blocks)
    near = [[8 * x + other for other in range(8)] for x in range(2)]
    share = lax.all_to_all(jnp.broadcast_to(share[None], (8,) + share.shape), "dp", 0, 0, axis_index_groups=near)
    share = jnp.sum(share.astype(F32), axis=0).astype(BF16)
    proto_unit_grad = blocks.T
    grad_proj = share.astype(F32) + swapped(share, "dp", 8).astype(F32)

    count = protos // lax.axis_size("dp")
    own_start = lax.axis_index("dp") * count
    own_unit, own_factor = unit_rows(
        lax.dynamic_slice_in_dim(prototypes, own_start, count, 0).astype(F32)
    )
    grad_protos = own_factor * (
        proto_unit_grad - own_unit * jnp.sum(own_unit * proto_unit_grad, axis=1, keepdims=True)
    )
    teacher_next = MOMENTUM * teacher_proj + (1.0 - MOMENTUM) * student_proj.astype(F32)
    return (crop_loss, grad_proj, grad_protos, teacher_next)


def solution(mesh):
    placed = (
        P("dp", "proto"),
        P("dp", "proto"),
        P(),
        P(),
        P("proto", None),
        P("proto", None),
        P("proto", None),
        P("dp"),
    )
    return jax.shard_map(
        body,
        mesh=mesh,
        in_specs=placed,
        out_specs=(P("dp"), P("proto", None), P(("proto", "dp"), None), P("proto", None)),
        check_vma=False,
    )
```

```python
import jax
import jax.numpy as jnp
from jax import lax
from jax.experimental import pallas as pl
from jax.experimental.pallas import tpu as pltpu
from jax.sharding import PartitionSpec as P

D = 1536
ITERS = 3


EPSILON = 1e-06
TEACHER_TEMP = 0.07
STUDENT_TEMP = 0.1
MOMENTUM = 0.994
BF16 = jnp.bfloat16
F32 = jnp.float32
LOG2E = 1.4426950408889634
BLOCK = 1024
GRANT = 16 * 1024 * 1024
LANES = 128


def contract_last(left, right):
    return lax.dot_general(left, right, (((1,), (1,)), ((), ())), preferred_element_type=F32)


def contract_first(left, right):
    return lax.dot_general(left, right, (((0,), (0,)), ((), ())), preferred_element_type=F32)


def unit_rows(values):
    factor = lax.rsqrt(jnp.sum(values * values, axis=1, keepdims=True) + EPSILON)
    return (values * factor, factor)


def exchanged(blocks, axis):
    return lax.all_to_all(blocks, axis, 0, 0)


def from_all(value, axis):
    count = lax.axis_size(axis)
    return exchanged(jnp.broadcast_to(value[None], (count,) + value.shape), axis)


def three_terms(value):
    high = value.astype(BF16)
    rest = value - high.astype(F32)
    middle = rest.astype(BF16)
    low = (rest - middle.astype(F32)).astype(BF16)
    return high, middle, low


def swapped(value, axis, bit):
    count = lax.axis_size(axis)
    return lax.ppermute(value, axis, [(one, one ^ bit) for one in range(count)])


def partial_hidden(features, gain, weight):
    scaled = (gain[:, None] * weight.astype(BF16).astype(F32)).astype(BF16)
    share = jnp.dot(features, scaled, preferred_element_type=F32)
    column = jnp.sum(scaled.astype(F32), axis=0)
    values = features.astype(F32)
    return share, column, jnp.sum(values, axis=1), jnp.sum(values * values, axis=1)


def center_and_scale(first, second):
    center = first / D
    return center, lax.rsqrt(second / D - center * center + EPSILON)


def packed_shares(features, gain, weight, parts):
    crops, size = features.shape[0], weight.shape[1]
    own = crops // parts
    share, column, first, second = partial_hidden(features, gain, weight)
    sums = jnp.stack(three_terms(jnp.stack([first, second])))
    sums = sums.reshape(6, parts, own).transpose(1, 0, 2).reshape(parts, 1, 6 * own)
    sums = jnp.pad(sums, ((0, 0), (0, 0), (0, size - 6 * own)))
    columns = jnp.broadcast_to(jnp.stack(three_terms(column))[None], (parts, 3, size))
    return jnp.concatenate([share.astype(BF16).reshape(parts, own, size), columns, sums], 1)


def summed_hidden(packed):
    own = packed.shape[1] - 4
    packed = jnp.sum(packed.astype(F32), axis=0)
    sums = jnp.sum(packed[own + 3, : 6 * own].reshape(3, 2, own), axis=0)
    center, scale = center_and_scale(sums[0][:, None], sums[1][:, None])
    column = jnp.sum(packed[own : own + 3], axis=0)[None]
    return scale * (packed[:own] - center * column)


def column_form(rows):
    return jnp.concatenate(
        [jnp.transpose(jnp.broadcast_to(rows[q : q + 1], (LANES, LANES))) for q in range(rows.shape[0])], 0
    )


def row_form(partial):
    return jnp.concatenate(
        [
            jnp.sum(jnp.transpose(partial[q * LANES : (q + 1) * LANES]), axis=0, keepdims=True)
            for q in range(partial.shape[0] // LANES)
        ],
        0,
    )


def stack_sum(ref):
    total = ref[0].astype(F32)
    for one in range(1, ref.shape[0]):
        total = total + ref[one].astype(F32)
    return total


def energy_kernel(teacher_ref, protos_ref, energy_ref, sums_ref, held):
    step = pl.program_id(0)
    rows = []
    for part in range(BLOCK // 256):
        cut = slice(part * 256, part * 256 + 256)
        value = jnp.exp2(contract_last(teacher_ref[...], protos_ref[cut, :]) * (LOG2E / TEACHER_TEMP))
        energy_ref[:, cut] = value.astype(BF16)
        total = jnp.sum(value, axis=0, keepdims=True)
        rows += [total[:, :LANES], total[:, LANES:]]
    held[pl.ds(pl.multiple_of(step * 8, 8), 8), :] = jnp.concatenate(rows, 0)

    @pl.when(step == pl.num_programs(0) - 1)
    def _():
        for one in range(sums_ref.shape[0]):
            sums_ref[one] = held[...].astype(BF16)


def row_kernel(got_ref, energy_ref, sums_ref, scale, held):
    step = pl.program_id(0)

    @pl.when(step == 0)
    def _():
        scale[...] = 1.0 / stack_sum(got_ref)
        held[...] = jnp.zeros_like(held)

    start = step * 8
    for low in range(0, held.shape[0], LANES):
        cut = slice(low, low + LANES)
        total = held[cut, :]
        for tile in range(8):
            total = total + energy_ref[cut, tile * LANES : (tile + 1) * LANES].astype(F32) * scale[pl.ds(start + tile, 1), :]
        held[cut, :] = total

    @pl.when(step == pl.num_programs(0) - 1)
    def _():
        total = row_form(held[...])
        for one in range(sums_ref.shape[0]):
            sums_ref[one] = total


def col_kernel(got_ref, energy_ref, sums_ref, scale, held):
    step = pl.program_id(0)

    @pl.when(step == 0)
    def _():
        scale[...] = column_form(1.0 / stack_sum(got_ref))

    rows = []
    for tile in range(8):
        value = energy_ref[:, tile * LANES : (tile + 1) * LANES].astype(F32) * scale[...]
        rows.append(jnp.sum(value, axis=0, keepdims=True))
    held[pl.ds(pl.multiple_of(step * 8, 8), 8), :] = jnp.concatenate(rows, 0)

    @pl.when(step == pl.num_programs(0) - 1)
    def _():
        for one in range(sums_ref.shape[0]):
            sums_ref[one] = held[...].astype(BF16)


def student_kernel(student_ref, protos_ref, exponent_ref, pulled_ref, partition_ref, held):
    step = pl.program_id(0)

    @pl.when(step == 0)
    def _():
        held[...] = jnp.zeros_like(held)
        pulled_ref[...] = jnp.zeros_like(pulled_ref)

    for part in range(BLOCK // 256):
        cut = slice(part * 256, part * 256 + 256)
        value = jnp.exp2(contract_last(student_ref[...], protos_ref[cut, :]) * (LOG2E / STUDENT_TEMP))
        held[...] += value[:, :LANES] + value[:, LANES:]
        exponent_ref[:, cut] = value.astype(BF16)
    pulled_ref[...] += jnp.dot(exponent_ref[...], protos_ref[...], preferred_element_type=F32)

    @pl.when(step == pl.num_programs(0) - 1)
    def _():
        partition_ref[...] = row_form(held[...])


def last_kernel(got_ref, partition_ref, energy_ref, student_ref, protos_ref, sums_ref, coded_ref, scale_ref, held, scaled):
    step = pl.program_id(0)

    @pl.when(step == 0)
    def _():
        scale_ref[...] = 1.0 / stack_sum(got_ref)
        held[...] = jnp.zeros_like(held)
        coded_ref[...] = jnp.zeros_like(coded_ref)

    start = step * 8
    for part in range(BLOCK // 256):
        left = energy_ref[:, part * 256 : part * 256 + LANES].astype(F32) * scale_ref[pl.ds(start + 2 * part, 1), :]
        right = energy_ref[:, part * 256 + LANES : part * 256 + 256].astype(F32) * scale_ref[pl.ds(start + 2 * part + 1, 1), :]
        held[...] += left + right
        scaled[:, part * 256 : part * 256 + LANES] = left.astype(BF16)
        scaled[:, part * 256 + LANES : part * 256 + 256] = right.astype(BF16)
    coded_ref[...] += jnp.dot(scaled[...], protos_ref[...], preferred_element_type=F32)

    @pl.when(step == pl.num_programs(0) - 1)
    def _():
        value = student_ref[...].astype(F32) * coded_ref[...]
        expected = value[:, :LANES]
        for tile in range(1, value.shape[1] // LANES):
            expected = expected + value[:, tile * LANES : (tile + 1) * LANES]
        total = jnp.concatenate(
            [row_form(held[...]), partition_ref[...], row_form(expected) * (1.0 / STUDENT_TEMP)], 0
        )
        for one in range(sums_ref.shape[0]):
            sums_ref[one] = total


def proto_block(line, turned_ref, wanted_ref, given_ref, scale_ref, exponent_ref, energy_ref):
    parts = []
    for half in range(2):
        cut = slice(half * LANES, half * LANES + LANES)
        scale = scale_ref[pl.ds(line + half, 1), :]
        score = exponent_ref[:, cut].astype(F32) * wanted_ref[...] - energy_ref[:, cut].astype(F32) * scale * given_ref[...]
        parts.append(score.astype(BF16))
    return jnp.dot(turned_ref[...], jnp.concatenate(parts, 1), preferred_element_type=F32)


def unit_grad_kernel(
    core_ref, got_ref, pulled_ref, coded_ref, turned_ref, scale_ref, exponent_ref, energy_ref,
    grad_ref, loss_ref, wanted_ref, given_ref, out_ref,
):
    @pl.when(pl.program_id(0) == 0)
    def _():
        total = stack_sum(got_ref)
        count = total.shape[0] // 3
        row = 1.0 / total[:count]
        partition = total[count : 2 * count]
        loss_ref[...] = jnp.log(partition) - total[2 * count :] * row
        wanted = column_form(1.0 / (partition * STUDENT_TEMP))
        given = column_form(row * (1.0 / STUDENT_TEMP))
        wanted_ref[...] = wanted
        given_ref[...] = given
        for tile in range(pulled_ref.shape[1] // LANES):
            cut = slice(tile * LANES, (tile + 1) * LANES)
            grad_ref[:, cut] = (pulled_ref[:, cut] * wanted - coded_ref[:, cut] * given).astype(BF16)

    line = pl.program_id(0) * 4 + core_ref[0] * 2
    value = proto_block(line, turned_ref, wanted_ref, given_ref, scale_ref, exponent_ref, energy_ref)
    out_ref[0] = value.astype(BF16)


def proto_grad_kernel(core_ref, turned_ref, wanted_ref, given_ref, scale_ref, exponent_ref, energy_ref, out_ref):
    line = pl.program_id(0) * 4 + core_ref[0] * 2
    value = proto_block(line, turned_ref, wanted_ref, given_ref, scale_ref, exponent_ref, energy_ref)
    out_ref[0] = value.astype(BF16)


def pair_sum_kernel(place_ref, kept_ref, got_ref, *out_refs):
    value = (kept_ref[:, 0].astype(F32) + got_ref[:, 0].astype(F32)).astype(BF16)
    for turn, out_ref in enumerate(out_refs):

        @pl.when(pl.program_id(0) == turn)
        def _():
            out_ref[...] = value


def hidden_grad_kernel(got_ref, unit_ref, factor_ref, out_ref):
    grad = stack_sum(got_ref)
    unit = unit_ref[...]
    grad = factor_ref[...] * (grad - unit * jnp.sum(unit * grad, axis=1, keepdims=True))
    grad = grad.astype(BF16)
    for one in range(out_ref.shape[0]):
        out_ref[one] = grad


def whole(shape):
    return pl.BlockSpec(shape, lambda step: (0,) * len(shape))


def called(kernel, steps, ins, outs, scratch, flops=0, moved=0, exps=0):
    return pl.pallas_call(
        kernel,
        grid=(steps,),
        in_specs=ins,
        out_specs=[spec for _, spec in outs],
        out_shape=[shape for shape, _ in outs],
        scratch_shapes=scratch,
        compiler_params=pltpu.CompilerParams(
            dimension_semantics=("arbitrary",), vmem_limit_bytes=GRANT
        ),
        cost_estimate=pl.CostEstimate(flops=flops, bytes_accessed=moved, transcendentals=exps),
    )


def array(shape, dtype):
    return jax.ShapeDtypeStruct(shape, dtype)


def make_calls(crops, protos, size, dps, parts):
    steps = protos // BLOCK
    lines, tiles = crops // LANES, protos // LANES
    across = pl.BlockSpec((crops, BLOCK), lambda step: (0, step))
    down = pl.BlockSpec((BLOCK, size), lambda step: (step, 0))
    matrix = crops * protos
    product = 2 * matrix * size
    col_sent = (array((dps, tiles, LANES), BF16), whole((dps, tiles, LANES)))
    row_sent = (array((parts, lines, LANES), F32), whole((parts, lines, LANES)))
    tall = pltpu.VMEM((crops, LANES), F32)
    short = pltpu.VMEM((tiles, LANES), F32)
    energy = called(
        energy_kernel, steps, [whole((crops, size)), down],
        [(array((crops, protos), BF16), across), col_sent],
        [short], product, 2 * matrix, matrix,
    )
    rows = called(
        row_kernel, steps, [whole((dps, tiles, LANES)), across], [row_sent], [short, tall], 2 * matrix, 2 * matrix
    )
    cols = called(
        col_kernel, steps, [whole((parts, lines, LANES)), across], [col_sent], [tall, short], 2 * matrix, 2 * matrix
    )
    student = called(
        student_kernel, steps, [whole((crops, size)), down],
        [
            (array((crops, protos), BF16), across),
            (array((crops, size), F32), whole((crops, size))),
            (array((lines, LANES), F32), whole((lines, LANES))),
        ],
        [tall], 2 * product, 2 * matrix, matrix,
    )
    last = called(
        last_kernel, steps,
        [whole((dps, tiles, LANES)), whole((lines, LANES)), across, whole((crops, size)), down],
        [
            (array((parts, 3 * lines, LANES), F32), whole((parts, 3 * lines, LANES))),
            (array((crops, size), F32), whole((crops, size))),
            (array((tiles, LANES), F32), whole((tiles, LANES))),
        ],
        [tall, pltpu.VMEM((crops, BLOCK), BF16)], product, 2 * matrix,
    )
    own = crops // parts
    hidden_grad = called(
        hidden_grad_kernel, 1, [whole((parts, own, size)), whole((own, size)), whole((own, 1))],
        [(array((parts, own, size), BF16), whole((parts, own, size)))], [], 6 * own * size, 4 * crops * size,
    )
    wide = protos // dps
    one = pl.BlockSpec((crops, wide), lambda step, core: (0, 2 * step + core[0]))
    out = pl.BlockSpec((1, size, wide), lambda step, core: (step, 0, 0))
    params = pltpu.CompilerParams(dimension_semantics=("arbitrary",), vmem_limit_bytes=GRANT)
    cost = pl.CostEstimate(flops=product // 2, bytes_accessed=2 * matrix + protos * size, transcendentals=0)

    def fixed(shape):
        return pl.BlockSpec(shape, lambda step, core: (0,) * len(shape))

    proto_grad = pl.pallas_call(
        proto_grad_kernel,
        grid_spec=pltpu.PrefetchScalarGridSpec(
            num_scalar_prefetch=1,
            grid=(dps // 2,),
            in_specs=[fixed((size, crops)), fixed((crops, LANES)), fixed((crops, LANES)), fixed((tiles, LANES)), one, one],
            out_specs=out,
        ),
        out_shape=array((dps // 2, size, wide), BF16),
        compiler_params=params,
        cost_estimate=cost,
    )
    turned = pl.BlockSpec((2, 1, size, wide), lambda step, place: (0, (place[0] + step) % 4, 0, 0))
    pair_sum = pl.pallas_call(
        pair_sum_kernel,
        grid_spec=pltpu.PrefetchScalarGridSpec(
            num_scalar_prefetch=1,
            grid=(4,),
            in_specs=[turned, turned],
            out_specs=[fixed((2, size, wide)) for _ in range(4)],
        ),
        out_shape=[array((2, size, wide), BF16) for _ in range(4)],
        compiler_params=params,
        cost_estimate=pl.CostEstimate(flops=protos * size, bytes_accessed=3 * protos * size, transcendentals=0),
    )
    unit_grad = pl.pallas_call(
        unit_grad_kernel,
        grid_spec=pltpu.PrefetchScalarGridSpec(
            num_scalar_prefetch=1,
            grid=(dps // 2,),
            in_specs=[
                fixed((parts, 3 * lines, LANES)), fixed((crops, size)), fixed((crops, size)),
                fixed((size, crops)), fixed((tiles, LANES)), one, one,
            ],
            out_specs=[fixed((crops, size)), fixed((lines, LANES)), fixed((crops, LANES)), fixed((crops, LANES)), out],
        ),
        out_shape=[
            array((crops, size), BF16), array((lines, LANES), F32), array((crops, LANES), F32),
            array((crops, LANES), F32), array((dps // 2, size, wide), BF16),
        ],
        compiler_params=params,
        cost_estimate=cost,
    )
    return energy, rows, cols, student, last, unit_grad, hidden_grad, proto_grad, pair_sum


def along_y(value, step):
    return lax.ppermute(value, "dp", [(one, (one & 9) | ((one + 2 * step) & 6)) for one in range(16)])


def body(
    student_cls,
    teacher_cls,
    student_gain,
    teacher_gain,
    student_proj,
    teacher_proj,
    prototypes,
    partner,
):
    crops, width = student_cls.shape
    parts = lax.axis_size("proto")
    own = crops // parts
    size = student_proj.shape[1]
    start = lax.axis_index("proto") * width
    opposite = swapped(student_cls, "dp", 8)
    gain_s = lax.dynamic_slice_in_dim(student_gain, start, width)
    gain_t = lax.dynamic_slice_in_dim(teacher_gain, start, width)

    teacher_blocks = packed_shares(teacher_cls, gain_t, teacher_proj, parts)
    teacher_hidden = summed_hidden(exchanged(teacher_blocks, "proto"))
    teacher_unit = unit_rows(teacher_hidden)[0].astype(BF16)
    teacher_all = from_all(teacher_unit, "proto").reshape(crops, size)

    pick = partner[:, None] % crops == jnp.arange(crops, dtype=jnp.int32)[None]
    turned = lax.dot_general(
        opposite, pick.astype(BF16), (((0,), (1,)), ((), ())), preferred_element_type=F32
    ).astype(BF16)
    weight = (gain_s[:, None] * student_proj.astype(F32)).astype(BF16)
    gathered = lax.all_gather(jnp.concatenate([turned, weight], 1), "proto", axis=0, tiled=True)

    proto_unit32, proto_factor = unit_rows(prototypes.astype(F32))
    proto_unit = proto_unit32.astype(BF16)
    protos = proto_unit.shape[0]
    calls = make_calls(crops, protos, size, lax.axis_size("dp"), parts)
    energy_call, row_call, col_call, student_call, last_call = calls[:5]
    unit_grad_call, hidden_grad_call, proto_grad_call, pair_sum_call = calls[5:]
    me = lax.axis_index("dp")
    count = protos // lax.axis_size("dp")
    across = me // 8
    places = (
        (1 - me % 2).reshape(1),
        (me % 2).reshape(1),
        ((me // 2) % 4).reshape(1),
        *(value.astype(jnp.uint32) for value in (lax.axis_index("proto") * own, across, 1 - across, me * count)),
    )
    energy, sums = energy_call(teacher_all, proto_unit)
    sums, places = lax.optimization_barrier((sums, places))
    other, core, place, own_at, kept_at, given_at, protos_at = places
    for step in range(ITERS - 1):
        (sums,) = row_call(exchanged(sums, "dp"), energy)
        (sums,) = col_call(exchanged(sums, "proto"), energy)
    sums, gathered, turned = lax.optimization_barrier((sums, gathered, turned))
    values = gathered[:, :crops].astype(F32)
    student_center, student_scale = center_and_scale(
        jnp.sum(values, axis=0)[:, None], jnp.sum(values * values, axis=0)[:, None]
    )
    weight = gathered[:, crops:]
    student_hidden = student_scale * (
        contract_first(gathered[:, :crops], weight) - student_center * jnp.sum(weight.astype(F32), axis=0)[None]
    )
    student_unit32, student_factor = unit_rows(student_hidden)
    student_unit = student_unit32.astype(BF16)
    normed = turned.astype(F32) - student_center.reshape(1, crops)
    normed = (normed * student_scale.reshape(1, crops) * gain_s[:, None]).astype(BF16)
    student_unit32, student_factor = (
        lax.dynamic_slice(value, (own_at, jnp.uint32(0)), (own, value.shape[1]))
        for value in (student_unit32, student_factor)
    )
    fields = student_call(student_unit, proto_unit)
    student = (student_unit, student_unit32, student_factor, normed, student_unit.T)
    sums, fields, student = lax.optimization_barrier((sums, fields, student))
    student_unit, student_unit32, student_factor, normed, turned_unit = student
    exponent, pulled, partition = fields
    sums = exchanged(sums, "dp")
    sums, coded, scale = last_call(sums, partition, energy, student_unit, proto_unit)
    unit_grad, crop_loss, wanted, given, give = unit_grad_call(
        other, exchanged(sums, "proto"), pulled, coded, turned_unit, scale, exponent, energy
    )
    give, unit_grad, crop_loss, prototypes = lax.optimization_barrier((give, unit_grad, crop_loss, prototypes))
    got = swapped(give, "dp", 1)
    unit_grad = exchanged(unit_grad.reshape(parts, own, size), "proto")
    kept = proto_grad_call(core, turned_unit, wanted, given, scale, exponent, energy)
    quads = (2, 4) + kept.shape[1:]
    blocks = pair_sum_call(place, kept.reshape(quads), got.reshape(quads))
    crop_loss = swapped(crop_loss, "dp", 8).reshape(1, crops)
    crop_loss = jnp.sum(jnp.where(pick, crop_loss, 0.0), axis=1)
    (sent,) = hidden_grad_call(unit_grad, student_unit32, student_factor)
    sent, blocks = lax.optimization_barrier((sent, blocks))
    sent = exchanged(sent, "proto").reshape(crops, size)
    share = jnp.dot(normed, sent, preferred_element_type=F32).astype(BF16)
    far = along_y(blocks[2], 2)
    share, far = lax.optimization_barrier((share, far))
    near = [[8 * x + other for other in range(8)] for x in range(2)]
    share = lax.all_to_all(jnp.broadcast_to(share[None], (8,) + share.shape), "dp", 0, 0, axis_index_groups=near)
    terms = (blocks[0], along_y(blocks[1], 1), along_y(blocks[3], 3), far)
    share, terms = lax.optimization_barrier((share, terms))
    total = sum(term.astype(F32) for term in terms).astype(BF16)
    keep, give = (
        lax.dynamic_slice(total, (at, jnp.uint32(0), jnp.uint32(0)), (1,) + total.shape[1:])[0]
        for at in (kept_at, given_at)
    )
    share = jnp.sum(share.astype(F32), axis=0).astype(BF16)
    proto_unit_grad = (keep.astype(F32) + swapped(give, "dp", 8).astype(F32)).T
    grad_proj = share.astype(F32) + swapped(share, "dp", 8).astype(F32)

    own_protos = lax.dynamic_slice(prototypes, (protos_at, jnp.uint32(0)), (count, size))
    own_unit, own_factor = unit_rows(own_protos.astype(F32))
    grad_protos = own_factor * (
        proto_unit_grad - own_unit * jnp.sum(own_unit * proto_unit_grad, axis=1, keepdims=True)
    )
    teacher_next = MOMENTUM * teacher_proj + (1.0 - MOMENTUM) * student_proj.astype(F32)
    return (crop_loss, grad_proj, grad_protos, teacher_next)


def solution(mesh):
    placed = (
        P("dp", "proto"),
        P("dp", "proto"),
        P(),
        P(),
        P("proto", None),
        P("proto", None),
        P("proto", None),
        P("dp"),
    )
    return jax.shard_map(
        body,
        mesh=mesh,
        in_specs=placed,
        out_specs=(P("dp"), P("proto", None), P(("proto", "dp"), None), P("proto", None)),
        check_vma=False,
    )
```

```python
import jax
import jax.numpy as jnp
from jax import lax
from jax.experimental import pallas as pl
from jax.experimental.pallas import tpu as pltpu
from jax.sharding import PartitionSpec as P

D = 1536
ITERS = 3


EPSILON = 1e-06
TEACHER_TEMP = 0.07
STUDENT_TEMP = 0.1
MOMENTUM = 0.994
BF16 = jnp.bfloat16
F32 = jnp.float32
LOG2E = 1.4426950408889634
BLOCK = 1024
GRANT = 16 * 1024 * 1024
LANES = 128


def contract_last(left, right):
    return lax.dot_general(left, right, (((1,), (1,)), ((), ())), preferred_element_type=F32)


def contract_first(left, right):
    return lax.dot_general(left, right, (((0,), (0,)), ((), ())), preferred_element_type=F32)


def unit_rows(values):
    factor = lax.rsqrt(jnp.sum(values * values, axis=1, keepdims=True) + EPSILON)
    return (values * factor, factor)


def exchanged(blocks, axis):
    return lax.all_to_all(blocks, axis, 0, 0)


def from_all(value, axis):
    count = lax.axis_size(axis)
    return exchanged(jnp.broadcast_to(value[None], (count,) + value.shape), axis)


def three_terms(value):
    high = value.astype(BF16)
    rest = value - high.astype(F32)
    middle = rest.astype(BF16)
    low = (rest - middle.astype(F32)).astype(BF16)
    return high, middle, low


def swapped(value, axis, bit):
    count = lax.axis_size(axis)
    return lax.ppermute(value, axis, [(one, one ^ bit) for one in range(count)])


def partial_hidden(features, gain, weight):
    scaled = (gain[:, None] * weight.astype(BF16).astype(F32)).astype(BF16)
    share = jnp.dot(features, scaled, preferred_element_type=F32)
    column = jnp.sum(scaled.astype(F32), axis=0)
    values = features.astype(F32)
    return share, column, jnp.sum(values, axis=1), jnp.sum(values * values, axis=1)


def center_and_scale(first, second):
    center = first / D
    return center, lax.rsqrt(second / D - center * center + EPSILON)


def packed_shares(features, gain, weight, parts):
    crops, size = features.shape[0], weight.shape[1]
    own = crops // parts
    share, column, first, second = partial_hidden(features, gain, weight)
    sums = jnp.stack(three_terms(jnp.stack([first, second])))
    sums = sums.reshape(6, parts, own).transpose(1, 0, 2).reshape(parts, 1, 6 * own)
    sums = jnp.pad(sums, ((0, 0), (0, 0), (0, size - 6 * own)))
    columns = jnp.broadcast_to(jnp.stack(three_terms(column))[None], (parts, 3, size))
    return jnp.concatenate([share.astype(BF16).reshape(parts, own, size), columns, sums], 1)


def summed_hidden(packed):
    own = packed.shape[1] - 4
    packed = jnp.sum(packed.astype(F32), axis=0)
    sums = jnp.sum(packed[own + 3, : 6 * own].reshape(3, 2, own), axis=0)
    center, scale = center_and_scale(sums[0][:, None], sums[1][:, None])
    column = jnp.sum(packed[own : own + 3], axis=0)[None]
    return scale * (packed[:own] - center * column)


def column_form(rows):
    return jnp.concatenate(
        [jnp.transpose(jnp.broadcast_to(rows[q : q + 1], (LANES, LANES))) for q in range(rows.shape[0])], 0
    )


def row_form(partial):
    return jnp.concatenate(
        [
            jnp.sum(jnp.transpose(partial[q * LANES : (q + 1) * LANES]), axis=0, keepdims=True)
            for q in range(partial.shape[0] // LANES)
        ],
        0,
    )


def stack_sum(ref):
    total = ref[0].astype(F32)
    for one in range(1, ref.shape[0]):
        total = total + ref[one].astype(F32)
    return total


def energy_kernel(teacher_ref, protos_ref, energy_ref, sums_ref, held):
    step = pl.program_id(0)
    rows = []
    for part in range(BLOCK // 256):
        cut = slice(part * 256, part * 256 + 256)
        value = jnp.exp2(contract_last(teacher_ref[...], protos_ref[cut, :]) * (LOG2E / TEACHER_TEMP))
        energy_ref[:, cut] = value.astype(BF16)
        total = jnp.sum(value, axis=0, keepdims=True)
        rows += [total[:, :LANES], total[:, LANES:]]
    held[pl.ds(pl.multiple_of(step * 8, 8), 8), :] = jnp.concatenate(rows, 0)

    @pl.when(step == pl.num_programs(0) - 1)
    def _():
        for one in range(sums_ref.shape[0]):
            sums_ref[one] = held[...].astype(BF16)


def row_kernel(got_ref, energy_ref, sums_ref, scale, held):
    step = pl.program_id(0)

    @pl.when(step == 0)
    def _():
        scale[...] = 1.0 / stack_sum(got_ref)
        held[...] = jnp.zeros_like(held)

    start = step * 8
    for low in range(0, held.shape[0], LANES):
        cut = slice(low, low + LANES)
        total = held[cut, :]
        for tile in range(8):
            total = total + energy_ref[cut, tile * LANES : (tile + 1) * LANES].astype(F32) * scale[pl.ds(start + tile, 1), :]
        held[cut, :] = total

    @pl.when(step == pl.num_programs(0) - 1)
    def _():
        total = row_form(held[...])
        for one in range(sums_ref.shape[0]):
            sums_ref[one] = total


def col_kernel(got_ref, energy_ref, sums_ref, scale, held):
    step = pl.program_id(0)

    @pl.when(step == 0)
    def _():
        scale[...] = column_form(1.0 / stack_sum(got_ref))

    rows = []
    for tile in range(8):
        value = energy_ref[:, tile * LANES : (tile + 1) * LANES].astype(F32) * scale[...]
        rows.append(jnp.sum(value, axis=0, keepdims=True))
    held[pl.ds(pl.multiple_of(step * 8, 8), 8), :] = jnp.concatenate(rows, 0)

    @pl.when(step == pl.num_programs(0) - 1)
    def _():
        for one in range(sums_ref.shape[0]):
            sums_ref[one] = held[...].astype(BF16)


def student_hidden_kernel(gathered_ref, own_ref, unit_ref, wide_ref, factor_ref, turned_ref, normed_ref):
    depth, crops = gathered_ref.shape[0], own_ref.shape[1]
    first = jnp.zeros((1, crops), F32)
    second = jnp.zeros((1, crops), F32)
    for low in range(0, depth, 64):
        part = gathered_ref[low : low + 64, :crops].astype(F32)
        first = first + jnp.sum(part, axis=0, keepdims=True)
        second = second + jnp.sum(part * part, axis=0, keepdims=True)
    center, scale = center_and_scale(first, second)
    normed_ref[...] = ((own_ref[...].astype(F32) - center) * scale).astype(BF16)
    column = jnp.sum(gathered_ref[:, crops:].astype(F32), axis=0, keepdims=True)
    wide_ref[...] = contract_first(gathered_ref[:, :crops], gathered_ref[:, crops:])

    def down(row):
        return jnp.concatenate([column_form(row[:, low : low + LANES]) for low in range(0, crops, LANES)], 0)

    center, scale = down(center), down(scale)
    cuts = [slice(low, low + LANES) for low in range(0, wide_ref.shape[1], LANES)]
    total = jnp.zeros((crops, LANES), F32)
    for cut in cuts:
        value = scale * (wide_ref[:, cut] - center * column[:, cut])
        wide_ref[:, cut] = value
        total = total + value * value
    factor = lax.rsqrt(jnp.sum(total, axis=1, keepdims=True) + EPSILON)
    factor_ref[...] = factor
    for cut in cuts:
        value = wide_ref[:, cut] * factor
        wide_ref[:, cut] = value
        unit_ref[:, cut] = value.astype(BF16)
        turned_ref[cut, :] = jnp.transpose(value).astype(BF16)


def student_kernel(student_ref, protos_ref, exponent_ref, pulled_ref, partition_ref, held):
    step = pl.program_id(0)

    @pl.when(step == 0)
    def _():
        held[...] = jnp.zeros_like(held)
        pulled_ref[...] = jnp.zeros_like(pulled_ref)

    for part in range(BLOCK // 256):
        cut = slice(part * 256, part * 256 + 256)
        value = jnp.exp2(contract_last(student_ref[...], protos_ref[cut, :]) * (LOG2E / STUDENT_TEMP))
        held[...] += value[:, :LANES] + value[:, LANES:]
        exponent_ref[:, cut] = value.astype(BF16)
    pulled_ref[...] += jnp.dot(exponent_ref[...], protos_ref[...], preferred_element_type=F32)

    @pl.when(step == pl.num_programs(0) - 1)
    def _():
        partition_ref[...] = row_form(held[...])


def last_kernel(got_ref, partition_ref, energy_ref, student_ref, protos_ref, sums_ref, coded_ref, scale_ref, held, scaled):
    step = pl.program_id(0)

    @pl.when(step == 0)
    def _():
        scale_ref[...] = 1.0 / stack_sum(got_ref)
        held[...] = jnp.zeros_like(held)
        coded_ref[...] = jnp.zeros_like(coded_ref)

    start = step * 8
    for part in range(BLOCK // 256):
        left = energy_ref[:, part * 256 : part * 256 + LANES].astype(F32) * scale_ref[pl.ds(start + 2 * part, 1), :]
        right = energy_ref[:, part * 256 + LANES : part * 256 + 256].astype(F32) * scale_ref[pl.ds(start + 2 * part + 1, 1), :]
        held[...] += left + right
        scaled[:, part * 256 : part * 256 + LANES] = left.astype(BF16)
        scaled[:, part * 256 + LANES : part * 256 + 256] = right.astype(BF16)
    coded_ref[...] += jnp.dot(scaled[...], protos_ref[...], preferred_element_type=F32)

    @pl.when(step == pl.num_programs(0) - 1)
    def _():
        value = student_ref[...].astype(F32) * coded_ref[...]
        expected = value[:, :LANES]
        for tile in range(1, value.shape[1] // LANES):
            expected = expected + value[:, tile * LANES : (tile + 1) * LANES]
        total = jnp.concatenate(
            [row_form(held[...]), partition_ref[...], row_form(expected) * (1.0 / STUDENT_TEMP)], 0
        )
        for one in range(sums_ref.shape[0]):
            sums_ref[one] = total


def proto_block(line, turned_ref, wanted_ref, given_ref, scale_ref, exponent_ref, energy_ref):
    parts = []
    for half in range(2):
        cut = slice(half * LANES, half * LANES + LANES)
        scale = scale_ref[pl.ds(line + half, 1), :]
        score = exponent_ref[:, cut].astype(F32) * wanted_ref[...] - energy_ref[:, cut].astype(F32) * scale * given_ref[...]
        parts.append(score.astype(BF16))
    return jnp.dot(turned_ref[...], jnp.concatenate(parts, 1), preferred_element_type=F32)


def unit_grad_kernel(
    core_ref, got_ref, pulled_ref, coded_ref, turned_ref, scale_ref, exponent_ref, energy_ref,
    grad_ref, loss_ref, wanted_ref, given_ref, out_ref,
):
    @pl.when(pl.program_id(0) == 0)
    def _():
        total = stack_sum(got_ref)
        count = total.shape[0] // 3
        row = 1.0 / total[:count]
        partition = total[count : 2 * count]
        loss_ref[...] = jnp.log(partition) - total[2 * count :] * row
        wanted = column_form(1.0 / (partition * STUDENT_TEMP))
        given = column_form(row * (1.0 / STUDENT_TEMP))
        wanted_ref[...] = wanted
        given_ref[...] = given
        for tile in range(pulled_ref.shape[1] // LANES):
            cut = slice(tile * LANES, (tile + 1) * LANES)
            grad_ref[:, cut] = (pulled_ref[:, cut] * wanted - coded_ref[:, cut] * given).astype(BF16)

    line = pl.program_id(0) * 4 + core_ref[0] * 2
    value = proto_block(line, turned_ref, wanted_ref, given_ref, scale_ref, exponent_ref, energy_ref)
    out_ref[0] = value.astype(BF16)


def proto_grad_kernel(core_ref, turned_ref, wanted_ref, given_ref, scale_ref, exponent_ref, energy_ref, out_ref):
    line = pl.program_id(0) * 4 + core_ref[0] * 2
    value = proto_block(line, turned_ref, wanted_ref, given_ref, scale_ref, exponent_ref, energy_ref)
    out_ref[0] = value.astype(BF16)


def pair_sum_kernel(place_ref, kept_ref, got_ref, *out_refs):
    value = (kept_ref[:, 0].astype(F32) + got_ref[:, 0].astype(F32)).astype(BF16)
    for turn, out_ref in enumerate(out_refs):

        @pl.when(pl.program_id(0) == turn)
        def _():
            out_ref[...] = value


def hidden_grad_kernel(got_ref, unit_ref, factor_ref, out_ref):
    grad = stack_sum(got_ref)
    unit = unit_ref[...]
    grad = factor_ref[...] * (grad - unit * jnp.sum(unit * grad, axis=1, keepdims=True))
    grad = grad.astype(BF16)
    for one in range(out_ref.shape[0]):
        out_ref[one] = grad


def whole(shape):
    return pl.BlockSpec(shape, lambda step: (0,) * len(shape))


def called(kernel, steps, ins, outs, scratch, flops=0, moved=0, exps=0):
    return pl.pallas_call(
        kernel,
        grid=(steps,),
        in_specs=ins,
        out_specs=[spec for _, spec in outs],
        out_shape=[shape for shape, _ in outs],
        scratch_shapes=scratch,
        compiler_params=pltpu.CompilerParams(
            dimension_semantics=("arbitrary",), vmem_limit_bytes=GRANT
        ),
        cost_estimate=pl.CostEstimate(flops=flops, bytes_accessed=moved, transcendentals=exps),
    )


def array(shape, dtype):
    return jax.ShapeDtypeStruct(shape, dtype)


def make_calls(crops, protos, size, dps, parts):
    steps = protos // BLOCK
    lines, tiles = crops // LANES, protos // LANES
    across = pl.BlockSpec((crops, BLOCK), lambda step: (0, step))
    down = pl.BlockSpec((BLOCK, size), lambda step: (step, 0))
    matrix = crops * protos
    product = 2 * matrix * size
    col_sent = (array((dps, tiles, LANES), BF16), whole((dps, tiles, LANES)))
    row_sent = (array((parts, lines, LANES), F32), whole((parts, lines, LANES)))
    tall = pltpu.VMEM((crops, LANES), F32)
    short = pltpu.VMEM((tiles, LANES), F32)
    energy = called(
        energy_kernel, steps, [whole((crops, size)), down],
        [(array((crops, protos), BF16), across), col_sent],
        [short], product, 2 * matrix, matrix,
    )
    rows = called(
        row_kernel, steps, [whole((dps, tiles, LANES)), across], [row_sent], [short, tall], 2 * matrix, 2 * matrix
    )
    cols = called(
        col_kernel, steps, [whole((parts, lines, LANES)), across], [col_sent], [tall, short], 2 * matrix, 2 * matrix
    )
    student = called(
        student_kernel, steps, [whole((crops, size)), down],
        [
            (array((crops, protos), BF16), across),
            (array((crops, size), F32), whole((crops, size))),
            (array((lines, LANES), F32), whole((lines, LANES))),
        ],
        [tall], 2 * product, 2 * matrix, matrix,
    )
    depth, width = D, D // parts
    student_hidden = called(
        student_hidden_kernel, 1, [whole((depth, crops + size)), whole((width, crops))],
        [
            (array((crops, size), BF16), whole((crops, size))),
            (array((crops, size), F32), whole((crops, size))),
            (array((crops, 1), F32), whole((crops, 1))),
            (array((size, crops), BF16), whole((size, crops))),
            (array((width, crops), BF16), whole((width, crops))),
        ],
        [], 2 * crops * depth * size, 2 * depth * (crops + size),
    )
    last = called(
        last_kernel, steps,
        [whole((dps, tiles, LANES)), whole((lines, LANES)), across, whole((crops, size)), down],
        [
            (array((parts, 3 * lines, LANES), F32), whole((parts, 3 * lines, LANES))),
            (array((crops, size), F32), whole((crops, size))),
            (array((tiles, LANES), F32), whole((tiles, LANES))),
        ],
        [tall, pltpu.VMEM((crops, BLOCK), BF16)], product, 2 * matrix,
    )
    own = crops // parts
    hidden_grad = called(
        hidden_grad_kernel, 1, [whole((parts, own, size)), whole((own, size)), whole((own, 1))],
        [(array((parts, own, size), BF16), whole((parts, own, size)))], [], 6 * own * size, 4 * crops * size,
    )
    wide = protos // dps
    one = pl.BlockSpec((crops, wide), lambda step, core: (0, 2 * step + core[0]))
    out = pl.BlockSpec((1, size, wide), lambda step, core: (step, 0, 0))
    params = pltpu.CompilerParams(dimension_semantics=("arbitrary",), vmem_limit_bytes=GRANT)
    cost = pl.CostEstimate(flops=product // 2, bytes_accessed=2 * matrix + protos * size, transcendentals=0)

    def fixed(shape):
        return pl.BlockSpec(shape, lambda step, core: (0,) * len(shape))

    proto_grad = pl.pallas_call(
        proto_grad_kernel,
        grid_spec=pltpu.PrefetchScalarGridSpec(
            num_scalar_prefetch=1,
            grid=(dps // 2,),
            in_specs=[fixed((size, crops)), fixed((crops, LANES)), fixed((crops, LANES)), fixed((tiles, LANES)), one, one],
            out_specs=out,
        ),
        out_shape=array((dps // 2, size, wide), BF16),
        compiler_params=params,
        cost_estimate=cost,
    )
    turned = pl.BlockSpec((2, 1, size, wide), lambda step, place: (0, (place[0] + step) % 4, 0, 0))
    pair_sum = pl.pallas_call(
        pair_sum_kernel,
        grid_spec=pltpu.PrefetchScalarGridSpec(
            num_scalar_prefetch=1,
            grid=(4,),
            in_specs=[turned, turned],
            out_specs=[fixed((2, size, wide)) for _ in range(4)],
        ),
        out_shape=[array((2, size, wide), BF16) for _ in range(4)],
        compiler_params=params,
        cost_estimate=pl.CostEstimate(flops=protos * size, bytes_accessed=3 * protos * size, transcendentals=0),
    )
    unit_grad = pl.pallas_call(
        unit_grad_kernel,
        grid_spec=pltpu.PrefetchScalarGridSpec(
            num_scalar_prefetch=1,
            grid=(dps // 2,),
            in_specs=[
                fixed((parts, 3 * lines, LANES)), fixed((crops, size)), fixed((crops, size)),
                fixed((size, crops)), fixed((tiles, LANES)), one, one,
            ],
            out_specs=[fixed((crops, size)), fixed((lines, LANES)), fixed((crops, LANES)), fixed((crops, LANES)), out],
        ),
        out_shape=[
            array((crops, size), BF16), array((lines, LANES), F32), array((crops, LANES), F32),
            array((crops, LANES), F32), array((dps // 2, size, wide), BF16),
        ],
        compiler_params=params,
        cost_estimate=cost,
    )
    return energy, rows, cols, student, last, unit_grad, hidden_grad, proto_grad, pair_sum, student_hidden


def along_y(value, step):
    return lax.ppermute(value, "dp", [(one, (one & 9) | ((one + 2 * step) & 6)) for one in range(16)])


def body(
    student_cls,
    teacher_cls,
    student_gain,
    teacher_gain,
    student_proj,
    teacher_proj,
    prototypes,
    partner,
):
    crops, width = student_cls.shape
    parts = lax.axis_size("proto")
    own = crops // parts
    size = student_proj.shape[1]
    start = lax.axis_index("proto") * width
    opposite = swapped(student_cls, "dp", 8)
    gain_s = lax.dynamic_slice_in_dim(student_gain, start, width)
    gain_t = lax.dynamic_slice_in_dim(teacher_gain, start, width)

    teacher_blocks = packed_shares(teacher_cls, gain_t, teacher_proj, parts)
    teacher_hidden = summed_hidden(exchanged(teacher_blocks, "proto"))
    teacher_unit = unit_rows(teacher_hidden)[0].astype(BF16)
    teacher_all = from_all(teacher_unit, "proto").reshape(crops, size)

    pick = partner[:, None] % crops == jnp.arange(crops, dtype=jnp.int32)[None]
    turned = lax.dot_general(
        opposite, pick.astype(BF16), (((0,), (1,)), ((), ())), preferred_element_type=F32
    ).astype(BF16)
    weight = (gain_s[:, None] * student_proj.astype(F32)).astype(BF16)
    gathered = lax.all_gather(jnp.concatenate([turned, weight], 1), "proto", axis=0, tiled=True)

    proto_unit32, proto_factor = unit_rows(prototypes.astype(F32))
    proto_unit = proto_unit32.astype(BF16)
    protos = proto_unit.shape[0]
    calls = make_calls(crops, protos, size, lax.axis_size("dp"), parts)
    energy_call, row_call, col_call, student_call, last_call = calls[:5]
    unit_grad_call, hidden_grad_call, proto_grad_call, pair_sum_call, student_hidden_call = calls[5:]
    me = lax.axis_index("dp")
    count = protos // lax.axis_size("dp")
    across = me // 8
    places = (
        (1 - me % 2).reshape(1),
        (me % 2).reshape(1),
        ((me // 2) % 4).reshape(1),
        *(value.astype(jnp.uint32) for value in (lax.axis_index("proto") * own, across, 1 - across, me * count)),
    )
    energy, sums = energy_call(teacher_all, proto_unit)
    sums, places = lax.optimization_barrier((sums, places))
    other, core, place, own_at, kept_at, given_at, protos_at = places
    for step in range(ITERS - 1):
        (sums,) = row_call(exchanged(sums, "dp"), energy)
        (sums,) = col_call(exchanged(sums, "proto"), energy)
    sums, gathered, turned = lax.optimization_barrier((sums, gathered, turned))
    student_unit, student_unit32, student_factor, turned_unit, normed = student_hidden_call(
        gathered, turned
    )
    fields = student_call(student_unit, proto_unit)
    sums, fields, turned_unit = lax.optimization_barrier((sums, fields, turned_unit))
    exponent, pulled, partition = fields
    sums = exchanged(sums, "dp")
    sums, coded, scale = last_call(sums, partition, energy, student_unit, proto_unit)
    unit_grad, crop_loss, wanted, given, give = unit_grad_call(
        other, exchanged(sums, "proto"), pulled, coded, turned_unit, scale, exponent, energy
    )
    give, unit_grad, crop_loss, own_at, protos_at = lax.optimization_barrier(
        (give, unit_grad, crop_loss, own_at, protos_at)
    )
    student_unit32, student_factor = (
        lax.dynamic_slice(value, (own_at, jnp.uint32(0)), (own, value.shape[1]))
        for value in (student_unit32, student_factor)
    )
    got = swapped(give, "dp", 1)
    unit_grad = exchanged(unit_grad.reshape(parts, own, size), "proto")
    kept = proto_grad_call(core, turned_unit, wanted, given, scale, exponent, energy)
    quads = (2, 4) + kept.shape[1:]
    blocks = pair_sum_call(place, kept.reshape(quads), got.reshape(quads))
    crop_loss = swapped(crop_loss, "dp", 8).reshape(1, crops)
    crop_loss = jnp.sum(jnp.where(pick, crop_loss, 0.0), axis=1)
    unit_grad, blocks = lax.optimization_barrier((unit_grad, blocks))
    (sent,) = hidden_grad_call(unit_grad, student_unit32, student_factor)
    sent = exchanged(sent, "proto").reshape(crops, size)
    share = (gain_s[:, None] * jnp.dot(normed, sent, preferred_element_type=F32)).astype(BF16)
    terms = (blocks[0], along_y(blocks[1], 1), along_y(blocks[2], 2), along_y(blocks[3], 3))
    share, terms = lax.optimization_barrier((share, terms))
    near = [[8 * x + other for other in range(8)] for x in range(2)]
    share = lax.all_to_all(jnp.broadcast_to(share[None], (8,) + share.shape), "dp", 0, 0, axis_index_groups=near)
    total = sum(term.astype(F32) for term in terms).astype(BF16)
    keep, give = (
        lax.dynamic_slice(total, (at, jnp.uint32(0), jnp.uint32(0)), (1,) + total.shape[1:])[0]
        for at in (kept_at, given_at)
    )
    share = jnp.sum(share.astype(F32), axis=0).astype(BF16)
    proto_unit_grad = (keep.astype(F32) + swapped(give, "dp", 8).astype(F32)).T
    grad_proj = share.astype(F32) + swapped(share, "dp", 8).astype(F32)

    own_protos = lax.dynamic_slice(prototypes, (protos_at, jnp.uint32(0)), (count, size))
    own_unit, own_factor = unit_rows(own_protos.astype(F32))
    grad_protos = own_factor * (
        proto_unit_grad - own_unit * jnp.sum(own_unit * proto_unit_grad, axis=1, keepdims=True)
    )
    teacher_next = MOMENTUM * teacher_proj + (1.0 - MOMENTUM) * student_proj.astype(F32)
    return (crop_loss, grad_proj, grad_protos, teacher_next)


def solution(mesh):
    placed = (
        P("dp", "proto"),
        P("dp", "proto"),
        P(),
        P(),
        P("proto", None),
        P("proto", None),
        P("proto", None),
        P("dp"),
    )
    return jax.shard_map(
        body,
        mesh=mesh,
        in_specs=placed,
        out_specs=(P("dp"), P("proto", None), P(("proto", "dp"), None), P("proto", None)),
        check_vma=False,
    )
```

```python
import jax
import jax.numpy as jnp
from jax import lax
from jax.experimental import pallas as pl
from jax.experimental.pallas import tpu as pltpu
from jax.sharding import PartitionSpec as P

D = 1536
ITERS = 3


EPSILON = 1e-06
TEACHER_TEMP = 0.07
STUDENT_TEMP = 0.1
MOMENTUM = 0.994
BF16 = jnp.bfloat16
F32 = jnp.float32
LOG2E = 1.4426950408889634
BLOCK = 1024
GRANT = 16 * 1024 * 1024
LANES = 128


def contract_last(left, right):
    return lax.dot_general(left, right, (((1,), (1,)), ((), ())), preferred_element_type=F32)


def contract_first(left, right):
    return lax.dot_general(left, right, (((0,), (0,)), ((), ())), preferred_element_type=F32)


def unit_rows(values):
    factor = lax.rsqrt(jnp.sum(values * values, axis=1, keepdims=True) + EPSILON)
    return (values * factor, factor)


def exchanged(blocks, axis):
    return lax.all_to_all(blocks, axis, 0, 0)


def from_all(value, axis):
    count = lax.axis_size(axis)
    return exchanged(jnp.broadcast_to(value[None], (count,) + value.shape), axis)


def three_terms(value):
    high = value.astype(BF16)
    rest = value - high.astype(F32)
    middle = rest.astype(BF16)
    low = (rest - middle.astype(F32)).astype(BF16)
    return high, middle, low


def swapped(value, axis, bit):
    count = lax.axis_size(axis)
    return lax.ppermute(value, axis, [(one, one ^ bit) for one in range(count)])


def center_and_scale(first, second):
    center = first / D
    return center, lax.rsqrt(second / D - center * center + EPSILON)


def summed_hidden(packed):
    own = packed.shape[1] - 5
    packed = jnp.sum(packed.astype(F32), axis=0)
    sums = jnp.sum(packed[own + 3 :].reshape(2, 3, LANES), axis=1)
    at = (lax.axis_index("proto") % (LANES // own) * own).astype(jnp.uint32)
    sums = lax.dynamic_slice(sums, (jnp.uint32(0), at), (2, own))
    center, scale = center_and_scale(sums[0][:, None], sums[1][:, None])
    column = jnp.sum(packed[own : own + 3], axis=0)[None]
    return scale * (packed[:own] - center * column)


def column_form(rows):
    return jnp.concatenate(
        [jnp.transpose(jnp.broadcast_to(rows[q : q + 1], (LANES, LANES))) for q in range(rows.shape[0])], 0
    )


def row_form(partial):
    return jnp.concatenate(
        [
            jnp.sum(jnp.transpose(partial[q * LANES : (q + 1) * LANES]), axis=0, keepdims=True)
            for q in range(partial.shape[0] // LANES)
        ],
        0,
    )


def stack_sum(ref):
    total = ref[0].astype(F32)
    for one in range(1, ref.shape[0]):
        total = total + ref[one].astype(F32)
    return total


def pack_kernel(features_ref, gain_ref, weight_ref, out_ref):
    scaled = (gain_ref[...] * weight_ref[...].astype(BF16).astype(F32)).astype(BF16)
    share = contract_first(features_ref[...], scaled)
    values = features_ref[...].astype(F32)
    columns, first, second = (
        [term.astype(F32) for term in three_terms(jnp.sum(one, axis=0, keepdims=True))]
        for one in (scaled.astype(F32), values, values * values)
    )
    parts = out_ref.shape[0]
    own = share.shape[0] // parts
    for part in range(parts):
        low = part * own // LANES * LANES
        lines = [jnp.concatenate([term[:, low : low + LANES] for term in terms], 1) for terms in (first, second)]
        block = jnp.concatenate([share[part * own : (part + 1) * own], *columns, *lines], 0)
        out_ref[part] = block.astype(BF16)


def energy_kernel(teacher_ref, protos_ref, energy_ref, sums_ref, held):
    step = pl.program_id(0)
    rows = []
    for part in range(BLOCK // 256):
        cut = slice(part * 256, part * 256 + 256)
        value = jnp.exp2(contract_last(teacher_ref[...], protos_ref[cut, :]) * (LOG2E / TEACHER_TEMP))
        energy_ref[:, cut] = value.astype(BF16)
        total = jnp.sum(value, axis=0, keepdims=True)
        rows += [total[:, :LANES], total[:, LANES:]]
    held[pl.ds(pl.multiple_of(step * 8, 8), 8), :] = jnp.concatenate(rows, 0)

    @pl.when(step == pl.num_programs(0) - 1)
    def _():
        for one in range(sums_ref.shape[0]):
            sums_ref[one] = held[...].astype(BF16)


def row_kernel(got_ref, energy_ref, sums_ref, scale, held):
    step = pl.program_id(0)

    @pl.when(step == 0)
    def _():
        scale[...] = 1.0 / stack_sum(got_ref)
        held[...] = jnp.zeros_like(held)

    start = step * 8
    for low in range(0, held.shape[0], LANES):
        cut = slice(low, low + LANES)
        total = held[cut, :]
        for tile in range(8):
            total = total + energy_ref[cut, tile * LANES : (tile + 1) * LANES].astype(F32) * scale[pl.ds(start + tile, 1), :]
        held[cut, :] = total

    @pl.when(step == pl.num_programs(0) - 1)
    def _():
        total = row_form(held[...])
        for one in range(sums_ref.shape[0]):
            sums_ref[one] = total


def col_kernel(got_ref, energy_ref, sums_ref, scale, held):
    step = pl.program_id(0)

    @pl.when(step == 0)
    def _():
        scale[...] = column_form(1.0 / stack_sum(got_ref))

    rows = []
    for tile in range(8):
        value = energy_ref[:, tile * LANES : (tile + 1) * LANES].astype(F32) * scale[...]
        rows.append(jnp.sum(value, axis=0, keepdims=True))
    held[pl.ds(pl.multiple_of(step * 8, 8), 8), :] = jnp.concatenate(rows, 0)

    @pl.when(step == pl.num_programs(0) - 1)
    def _():
        for one in range(sums_ref.shape[0]):
            sums_ref[one] = held[...].astype(BF16)


def student_hidden_kernel(gathered_ref, own_ref, unit_ref, wide_ref, factor_ref, turned_ref, normed_ref):
    depth, crops = gathered_ref.shape[0], own_ref.shape[1]
    first = jnp.zeros((1, crops), F32)
    second = jnp.zeros((1, crops), F32)
    for low in range(0, depth, 64):
        part = gathered_ref[low : low + 64, :crops].astype(F32)
        first = first + jnp.sum(part, axis=0, keepdims=True)
        second = second + jnp.sum(part * part, axis=0, keepdims=True)
    center, scale = center_and_scale(first, second)
    normed_ref[...] = ((own_ref[...].astype(F32) - center) * scale).astype(BF16)
    column = jnp.sum(gathered_ref[:, crops:].astype(F32), axis=0, keepdims=True)
    wide_ref[...] = contract_first(gathered_ref[:, :crops], gathered_ref[:, crops:])

    def down(row):
        return jnp.concatenate([column_form(row[:, low : low + LANES]) for low in range(0, crops, LANES)], 0)

    center, scale = down(center), down(scale)
    cuts = [slice(low, low + LANES) for low in range(0, wide_ref.shape[1], LANES)]
    total = jnp.zeros((crops, LANES), F32)
    for cut in cuts:
        value = scale * (wide_ref[:, cut] - center * column[:, cut])
        wide_ref[:, cut] = value
        total = total + value * value
    factor = lax.rsqrt(jnp.sum(total, axis=1, keepdims=True) + EPSILON)
    factor_ref[...] = factor
    for cut in cuts:
        value = wide_ref[:, cut] * factor
        wide_ref[:, cut] = value
        unit_ref[:, cut] = value.astype(BF16)
        turned_ref[cut, :] = jnp.transpose(value).astype(BF16)


def student_kernel(student_ref, protos_ref, exponent_ref, pulled_ref, partition_ref, held):
    step = pl.program_id(0)

    @pl.when(step == 0)
    def _():
        held[...] = jnp.zeros_like(held)
        pulled_ref[...] = jnp.zeros_like(pulled_ref)

    for part in range(BLOCK // 256):
        cut = slice(part * 256, part * 256 + 256)
        value = jnp.exp2(contract_last(student_ref[...], protos_ref[cut, :]) * (LOG2E / STUDENT_TEMP))
        held[...] += value[:, :LANES] + value[:, LANES:]
        exponent_ref[:, cut] = value.astype(BF16)
    pulled_ref[...] += jnp.dot(exponent_ref[...], protos_ref[...], preferred_element_type=F32)

    @pl.when(step == pl.num_programs(0) - 1)
    def _():
        partition_ref[...] = row_form(held[...])


def last_kernel(got_ref, partition_ref, energy_ref, student_ref, protos_ref, sums_ref, coded_ref, scale_ref, held, scaled):
    step = pl.program_id(0)

    @pl.when(step == 0)
    def _():
        scale_ref[...] = 1.0 / stack_sum(got_ref)
        held[...] = jnp.zeros_like(held)
        coded_ref[...] = jnp.zeros_like(coded_ref)

    start = step * 8
    for part in range(BLOCK // 256):
        left = energy_ref[:, part * 256 : part * 256 + LANES].astype(F32) * scale_ref[pl.ds(start + 2 * part, 1), :]
        right = energy_ref[:, part * 256 + LANES : part * 256 + 256].astype(F32) * scale_ref[pl.ds(start + 2 * part + 1, 1), :]
        held[...] += left + right
        scaled[:, part * 256 : part * 256 + LANES] = left.astype(BF16)
        scaled[:, part * 256 + LANES : part * 256 + 256] = right.astype(BF16)
    coded_ref[...] += jnp.dot(scaled[...], protos_ref[...], preferred_element_type=F32)

    @pl.when(step == pl.num_programs(0) - 1)
    def _():
        value = student_ref[...].astype(F32) * coded_ref[...]
        expected = value[:, :LANES]
        for tile in range(1, value.shape[1] // LANES):
            expected = expected + value[:, tile * LANES : (tile + 1) * LANES]
        total = jnp.concatenate(
            [row_form(held[...]), partition_ref[...], row_form(expected) * (1.0 / STUDENT_TEMP)], 0
        )
        for one in range(sums_ref.shape[0]):
            sums_ref[one] = total


def proto_block(line, turned_ref, wanted_ref, given_ref, scale_ref, exponent_ref, energy_ref):
    parts = []
    for half in range(2):
        cut = slice(half * LANES, half * LANES + LANES)
        scale = scale_ref[pl.ds(line + half, 1), :]
        score = exponent_ref[:, cut].astype(F32) * wanted_ref[...] - energy_ref[:, cut].astype(F32) * scale * given_ref[...]
        parts.append(score.astype(BF16))
    return jnp.dot(turned_ref[...], jnp.concatenate(parts, 1), preferred_element_type=F32)


def unit_grad_kernel(
    core_ref, got_ref, pulled_ref, coded_ref, turned_ref, scale_ref, exponent_ref, energy_ref,
    grad_ref, loss_ref, wanted_ref, given_ref, out_ref,
):
    @pl.when(pl.program_id(0) == 0)
    def _():
        total = stack_sum(got_ref)
        count = total.shape[0] // 3
        row = 1.0 / total[:count]
        partition = total[count : 2 * count]
        loss_ref[...] = jnp.log(partition) - total[2 * count :] * row
        wanted = column_form(1.0 / (partition * STUDENT_TEMP))
        given = column_form(row * (1.0 / STUDENT_TEMP))
        wanted_ref[...] = wanted
        given_ref[...] = given
        for tile in range(pulled_ref.shape[1] // LANES):
            cut = slice(tile * LANES, (tile + 1) * LANES)
            grad_ref[:, cut] = (pulled_ref[:, cut] * wanted - coded_ref[:, cut] * given).astype(BF16)

    line = pl.program_id(0) * 4 + core_ref[0] * 2
    value = proto_block(line, turned_ref, wanted_ref, given_ref, scale_ref, exponent_ref, energy_ref)
    out_ref[0] = value.astype(BF16)


def proto_grad_kernel(core_ref, turned_ref, wanted_ref, given_ref, scale_ref, exponent_ref, energy_ref, out_ref):
    line = pl.program_id(0) * 4 + core_ref[0] * 2
    value = proto_block(line, turned_ref, wanted_ref, given_ref, scale_ref, exponent_ref, energy_ref)
    out_ref[0] = value.astype(BF16)


def pair_sum_kernel(place_ref, kept_ref, got_ref, *out_refs):
    value = (kept_ref[:, 0].astype(F32) + got_ref[:, 0].astype(F32)).astype(BF16)
    for turn, out_ref in enumerate(out_refs):

        @pl.when(pl.program_id(0) == turn)
        def _():
            out_ref[...] = value


def hidden_grad_kernel(got_ref, unit_ref, factor_ref, out_ref):
    grad = stack_sum(got_ref)
    unit = unit_ref[...]
    grad = factor_ref[...] * (grad - unit * jnp.sum(unit * grad, axis=1, keepdims=True))
    grad = grad.astype(BF16)
    for one in range(out_ref.shape[0]):
        out_ref[one] = grad


def whole(shape):
    return pl.BlockSpec(shape, lambda step: (0,) * len(shape))


def called(kernel, steps, ins, outs, scratch, flops=0, moved=0, exps=0):
    return pl.pallas_call(
        kernel,
        grid=(steps,),
        in_specs=ins,
        out_specs=[spec for _, spec in outs],
        out_shape=[shape for shape, _ in outs],
        scratch_shapes=scratch,
        compiler_params=pltpu.CompilerParams(
            dimension_semantics=("arbitrary",), vmem_limit_bytes=GRANT
        ),
        cost_estimate=pl.CostEstimate(flops=flops, bytes_accessed=moved, transcendentals=exps),
    )


def array(shape, dtype):
    return jax.ShapeDtypeStruct(shape, dtype)


def make_calls(crops, protos, size, dps, parts):
    steps = protos // BLOCK
    lines, tiles = crops // LANES, protos // LANES
    across = pl.BlockSpec((crops, BLOCK), lambda step: (0, step))
    down = pl.BlockSpec((BLOCK, size), lambda step: (step, 0))
    matrix = crops * protos
    product = 2 * matrix * size
    col_sent = (array((dps, tiles, LANES), BF16), whole((dps, tiles, LANES)))
    row_sent = (array((parts, lines, LANES), F32), whole((parts, lines, LANES)))
    tall = pltpu.VMEM((crops, LANES), F32)
    short = pltpu.VMEM((tiles, LANES), F32)
    own, width = crops // parts, D // parts
    pack = called(
        pack_kernel, 1, [whole((width, crops)), whole((width, 1)), whole((width, size))],
        [(array((parts, own + 5, size), BF16), whole((parts, own + 5, size)))],
        [], 2 * crops * width * size, 2 * crops * size,
    )
    energy = called(
        energy_kernel, steps, [whole((crops, size)), down],
        [(array((crops, protos), BF16), across), col_sent],
        [short], product, 2 * matrix, matrix,
    )
    rows = called(
        row_kernel, steps, [whole((dps, tiles, LANES)), across], [row_sent], [short, tall], 2 * matrix, 2 * matrix
    )
    cols = called(
        col_kernel, steps, [whole((parts, lines, LANES)), across], [col_sent], [tall, short], 2 * matrix, 2 * matrix
    )
    student = called(
        student_kernel, steps, [whole((crops, size)), down],
        [
            (array((crops, protos), BF16), across),
            (array((crops, size), F32), whole((crops, size))),
            (array((lines, LANES), F32), whole((lines, LANES))),
        ],
        [tall], 2 * product, 2 * matrix, matrix,
    )
    depth, width = D, D // parts
    student_hidden = called(
        student_hidden_kernel, 1, [whole((depth, crops + size)), whole((width, crops))],
        [
            (array((crops, size), BF16), whole((crops, size))),
            (array((crops, size), F32), whole((crops, size))),
            (array((crops, 1), F32), whole((crops, 1))),
            (array((size, crops), BF16), whole((size, crops))),
            (array((width, crops), BF16), whole((width, crops))),
        ],
        [], 2 * crops * depth * size, 2 * depth * (crops + size),
    )
    last = called(
        last_kernel, steps,
        [whole((dps, tiles, LANES)), whole((lines, LANES)), across, whole((crops, size)), down],
        [
            (array((parts, 3 * lines, LANES), F32), whole((parts, 3 * lines, LANES))),
            (array((crops, size), F32), whole((crops, size))),
            (array((tiles, LANES), F32), whole((tiles, LANES))),
        ],
        [tall, pltpu.VMEM((crops, BLOCK), BF16)], product, 2 * matrix,
    )
    own = crops // parts
    hidden_grad = called(
        hidden_grad_kernel, 1, [whole((parts, own, size)), whole((own, size)), whole((own, 1))],
        [(array((parts, own, size), BF16), whole((parts, own, size)))], [], 6 * own * size, 4 * crops * size,
    )
    wide = protos // dps
    one = pl.BlockSpec((crops, wide), lambda step, core: (0, 2 * step + core[0]))
    out = pl.BlockSpec((1, size, wide), lambda step, core: (step, 0, 0))
    params = pltpu.CompilerParams(dimension_semantics=("arbitrary",), vmem_limit_bytes=GRANT)
    cost = pl.CostEstimate(flops=product // 2, bytes_accessed=2 * matrix + protos * size, transcendentals=0)

    def fixed(shape):
        return pl.BlockSpec(shape, lambda step, core: (0,) * len(shape))

    proto_grad = pl.pallas_call(
        proto_grad_kernel,
        grid_spec=pltpu.PrefetchScalarGridSpec(
            num_scalar_prefetch=1,
            grid=(dps // 2,),
            in_specs=[fixed((size, crops)), fixed((crops, LANES)), fixed((crops, LANES)), fixed((tiles, LANES)), one, one],
            out_specs=out,
        ),
        out_shape=array((dps // 2, size, wide), BF16),
        compiler_params=params,
        cost_estimate=cost,
    )
    turned = pl.BlockSpec((2, 1, size, wide), lambda step, place: (0, (place[0] + step) % 4, 0, 0))
    pair_sum = pl.pallas_call(
        pair_sum_kernel,
        grid_spec=pltpu.PrefetchScalarGridSpec(
            num_scalar_prefetch=1,
            grid=(4,),
            in_specs=[turned, turned],
            out_specs=[fixed((2, size, wide)) for _ in range(4)],
        ),
        out_shape=[array((2, size, wide), BF16) for _ in range(4)],
        compiler_params=params,
        cost_estimate=pl.CostEstimate(flops=protos * size, bytes_accessed=3 * protos * size, transcendentals=0),
    )
    unit_grad = pl.pallas_call(
        unit_grad_kernel,
        grid_spec=pltpu.PrefetchScalarGridSpec(
            num_scalar_prefetch=1,
            grid=(dps // 2,),
            in_specs=[
                fixed((parts, 3 * lines, LANES)), fixed((crops, size)), fixed((crops, size)),
                fixed((size, crops)), fixed((tiles, LANES)), one, one,
            ],
            out_specs=[fixed((crops, size)), fixed((lines, LANES)), fixed((crops, LANES)), fixed((crops, LANES)), out],
        ),
        out_shape=[
            array((crops, size), BF16), array((lines, LANES), F32), array((crops, LANES), F32),
            array((crops, LANES), F32), array((dps // 2, size, wide), BF16),
        ],
        compiler_params=params,
        cost_estimate=cost,
    )
    return energy, rows, cols, student, last, unit_grad, hidden_grad, proto_grad, pair_sum, student_hidden, pack


def along_y(value, step):
    return lax.ppermute(value, "dp", [(one, (one & 9) | ((one + 2 * step) & 6)) for one in range(16)])


def body(
    student_cls,
    teacher_cls,
    student_gain,
    teacher_gain,
    student_proj,
    teacher_proj,
    prototypes,
    partner,
):
    crops, width = student_cls.shape
    parts = lax.axis_size("proto")
    own = crops // parts
    size = student_proj.shape[1]
    start = lax.axis_index("proto") * width
    opposite = swapped(student_cls, "dp", 8)
    gain_s = lax.dynamic_slice_in_dim(student_gain, start, width)
    gain_t = lax.dynamic_slice_in_dim(teacher_gain, start, width)

    protos = prototypes.shape[0]
    calls = make_calls(crops, protos, size, lax.axis_size("dp"), parts)
    (teacher_blocks,) = calls[-1](teacher_cls.T, gain_t[:, None], teacher_proj)
    teacher_hidden = summed_hidden(exchanged(teacher_blocks, "proto"))
    teacher_unit = unit_rows(teacher_hidden)[0].astype(BF16)
    teacher_all = from_all(teacher_unit, "proto").reshape(crops, size)

    pick = partner[:, None] % crops == jnp.arange(crops, dtype=jnp.int32)[None]
    turned = lax.dot_general(
        opposite, pick.astype(BF16), (((0,), (1,)), ((), ())), preferred_element_type=F32
    ).astype(BF16)
    weight = (gain_s[:, None] * student_proj.astype(F32)).astype(BF16)
    gathered = lax.all_gather(jnp.concatenate([turned, weight], 1), "proto", axis=0, tiled=True)

    proto_unit32, proto_factor = unit_rows(prototypes.astype(F32))
    proto_unit = proto_unit32.astype(BF16)
    energy_call, row_call, col_call, student_call, last_call = calls[:5]
    unit_grad_call, hidden_grad_call, proto_grad_call, pair_sum_call, student_hidden_call = calls[5:-1]
    me = lax.axis_index("dp")
    count = protos // lax.axis_size("dp")
    across = me // 8
    places = (
        (1 - me % 2).reshape(1),
        (me % 2).reshape(1),
        ((me // 2) % 4).reshape(1),
        *(value.astype(jnp.uint32) for value in (lax.axis_index("proto") * own, across, 1 - across, me * count)),
    )
    energy, sums = energy_call(teacher_all, proto_unit)
    sums, places = lax.optimization_barrier((sums, places))
    other, core, place, own_at, kept_at, given_at, protos_at = places
    for step in range(ITERS - 1):
        (sums,) = row_call(exchanged(sums, "dp"), energy)
        (sums,) = col_call(exchanged(sums, "proto"), energy)
    sums, gathered, turned = lax.optimization_barrier((sums, gathered, turned))
    student_unit, student_unit32, student_factor, turned_unit, normed = student_hidden_call(
        gathered, turned
    )
    fields = student_call(student_unit, proto_unit)
    sums, fields, turned_unit = lax.optimization_barrier((sums, fields, turned_unit))
    exponent, pulled, partition = fields
    sums = exchanged(sums, "dp")
    sums, coded, scale = last_call(sums, partition, energy, student_unit, proto_unit)
    unit_grad, crop_loss, wanted, given, give = unit_grad_call(
        other, exchanged(sums, "proto"), pulled, coded, turned_unit, scale, exponent, energy
    )
    give, unit_grad, crop_loss, own_at, protos_at = lax.optimization_barrier(
        (give, unit_grad, crop_loss, own_at, protos_at)
    )
    student_unit32, student_factor = (
        lax.dynamic_slice(value, (own_at, jnp.uint32(0)), (own, value.shape[1]))
        for value in (student_unit32, student_factor)
    )
    got = swapped(give, "dp", 1)
    unit_grad = exchanged(unit_grad.reshape(parts, own, size), "proto")
    kept = proto_grad_call(core, turned_unit, wanted, given, scale, exponent, energy)
    quads = (2, 4) + kept.shape[1:]
    blocks = pair_sum_call(place, kept.reshape(quads), got.reshape(quads))
    crop_loss = swapped(crop_loss, "dp", 8).reshape(1, crops)
    crop_loss = jnp.sum(jnp.where(pick, crop_loss, 0.0), axis=1)
    unit_grad, blocks = lax.optimization_barrier((unit_grad, blocks))
    (sent,) = hidden_grad_call(unit_grad, student_unit32, student_factor)
    sent = exchanged(sent, "proto").reshape(crops, size)
    share = (gain_s[:, None] * jnp.dot(normed, sent, preferred_element_type=F32)).astype(BF16)
    terms = (blocks[0], along_y(blocks[1], 1), along_y(blocks[2], 2), along_y(blocks[3], 3))
    share, terms = lax.optimization_barrier((share, terms))
    near = [[8 * x + other for other in range(8)] for x in range(2)]
    share = lax.all_to_all(jnp.broadcast_to(share[None], (8,) + share.shape), "dp", 0, 0, axis_index_groups=near)
    total = sum(term.astype(F32) for term in terms).astype(BF16)
    keep, give = (
        lax.dynamic_slice(total, (at, jnp.uint32(0), jnp.uint32(0)), (1,) + total.shape[1:])[0]
        for at in (kept_at, given_at)
    )
    share = jnp.sum(share.astype(F32), axis=0).astype(BF16)
    proto_unit_grad = (keep.astype(F32) + swapped(give, "dp", 8).astype(F32)).T
    grad_proj = share.astype(F32) + swapped(share, "dp", 8).astype(F32)

    own_protos = lax.dynamic_slice(prototypes, (protos_at, jnp.uint32(0)), (count, size))
    own_unit, own_factor = unit_rows(own_protos.astype(F32))
    grad_protos = own_factor * (
        proto_unit_grad - own_unit * jnp.sum(own_unit * proto_unit_grad, axis=1, keepdims=True)
    )
    teacher_next = MOMENTUM * teacher_proj + (1.0 - MOMENTUM) * student_proj.astype(F32)
    return (crop_loss, grad_proj, grad_protos, teacher_next)


def solution(mesh):
    placed = (
        P("dp", "proto"),
        P("dp", "proto"),
        P(),
        P(),
        P("proto", None),
        P("proto", None),
        P("proto", None),
        P("dp"),
    )
    return jax.shard_map(
        body,
        mesh=mesh,
        in_specs=placed,
        out_specs=(P("dp"), P("proto", None), P(("proto", "dp"), None), P("proto", None)),
        check_vma=False,
    )
```
